128 devices in a mesh: section: 2 (over x_hi), dp: 16 (over y, x_lo, core), tensor: 4 (over z).
Axes of the slice: x: 4 (x_hi: 2, x_lo: 2; x = x_hi * 2 + x_lo), y: 4, z: 4, core: 2. Of those that a mesh axis runs over, the one named last changes fastest.
Arguments:
- boundary: bfloat16 [2, 2, 16, 576, 1024], P('section', None, 'dp', 'tensor'), may hold values from -6 to 6
- w_qkv: bfloat16 [2, 1024, 3, 1024], P('section', 'dp', None, 'tensor'), may hold values from -0.1875 to 0.1875
- qv_bias: bfloat16 [2, 2, 16, 64], P('section', None, 'tensor', 'dp'), may hold values from -3 to 3
- w_out: bfloat16 [2, 1024, 1024], P('section', 'tensor', 'dp'), may hold values from -1.5 to 1.5
- up_weight: bfloat16 [2, 1024, 4096], P('section', 'dp', 'tensor'), may hold values from -0.1875 to 0.1875
- up_bias: bfloat16 [2, 64, 64], P('section', 'tensor', 'dp'), may hold values from -3 to 3
- down_weight: bfloat16 [2, 4096, 1024], P('section', 'tensor', 'dp'), may hold values from -0.09375 to 0.09375
- norm_bias: bfloat16 [2, 6, 1024], P('section', None, ('dp', 'tensor')), as said below
Outputs:
- ends: float32 [2, 2, 16, 576, 1024], P('section', None, 'dp', 'tensor')
- grad_qkv: float32 [2, 1024, 3, 1024], P('section', 'dp', None, 'tensor')
- grad_qv_bias: float32 [2, 2, 16, 64], P('section', None, 'tensor', 'dp')
- grad_w_out: float32 [2, 1024, 1024], P('section', 'tensor', 'dp')
- grad_up_weight: float32 [2, 1024, 4096], P('section', 'dp', 'tensor')
- grad_up_bias: float32 [2, 64, 64], P('section', 'tensor', 'dp')
- grad_down_weight: float32 [2, 4096, 1024], P('section', 'tensor', 'dp')
- grad_norm_bias: float32 [2, 6, 1024], P('section', None, ('dp', 'tensor'))
The draws below stay inside these ranges and needn't reach their ends.
Inputs may be any that keep to these rules, and one draw needn't show every extreme that they name: Rows 0 and 3 of norm_bias lie within 0.4 to 1.6, the other rows within -0.9 to 0.9.
All inputs are finite; a program needn't handle non-finite values.
Results may differ from the reference program's by a relative error of at most 0.03.
Values may be sent and summed in bfloat16 or wider, within the bound.
A program may use at most 192 MiB of HBM per device.

```python
import jax
import jax.numpy as jnp
from jax import lax

D = 1024
HEADS = 16
HD = 64
FF = 4096
L = 576
MICRO = 2
IMAGES = 16
N_SECTION = 2


def draw_norm_bias(key, part):
    key = jax.random.fold_in(key, 7)
    gain_key, shift_key = jax.random.split(key)
    full_shape = (N_SECTION, 6, D)
    gains = jax.random.uniform(gain_key, full_shape, jnp.float32, 0.5, 1.5)
    shifts = jnp.clip(0.3 * jax.random.normal(shift_key, full_shape, jnp.float32), -0.9, 0.9)
    row_index = jnp.arange(6)[None, :, None]
    is_gain = (row_index == 0) | (row_index == 3)
    return jnp.where(is_gain, gains, shifts).astype(jnp.bfloat16)


def shard_levels(own_key, dims, cuts, least, top_value):
    level = 1.0
    for axis_at, parts in cuts:
        heights = jax.random.uniform(jax.random.fold_in(jax.random.fold_in(own_key, 6), axis_at), (parts,), jnp.float32, least / len(cuts), top_value / len(cuts))
        level = level * jnp.repeat(jnp.exp(heights), dims[axis_at] // parts).reshape((-1,) + (1,) * (len(dims) - 1 - axis_at))
    return level


def scatter_about(own_key, dims, scale, limit, pieces=(), held_as=jnp.bfloat16):
    entries = scale * jax.random.normal(own_key, dims, jnp.float32)
    if pieces:
        entries = entries * shard_levels(own_key, dims, pieces, -0.22, 0.18)
    return jnp.clip(entries, -limit, limit).astype(held_as)


def setup_inputs(seed: int = 0) -> dict:
    splits = jax.random.split(jax.random.key(seed), 9)
    return {
        "boundary": scatter_about(splits[0], (N_SECTION, MICRO, IMAGES, L, D), 1.0, 6.0, ((0, 2), (2, 16), (3, 4))),
        "w_qkv": scatter_about(splits[1], (N_SECTION, D, 3, D), D ** -0.5, 0.1875, ((0, 2), (1, 16), (3, 4))),
        "qv_bias": scatter_about(splits[2], (N_SECTION, 2, HEADS, HD), 0.5, 3.0, ((0, 2), (2, 4), (3, 16))),
        "w_out": scatter_about(splits[3], (N_SECTION, D, D), (D // 64) ** -0.5, 1.5, ((0, 2), (1, 4), (2, 16))),
        "up_weight": scatter_about(splits[4], (N_SECTION, D, FF), D ** -0.5, 0.1875, ((0, 2), (1, 16), (2, 4))),
        "up_bias": scatter_about(splits[5], (N_SECTION, FF // HD, HD), 0.5, 3.0, ((0, 2), (1, 4), (2, 16))),
        "down_weight": scatter_about(splits[6], (N_SECTION, FF, D), FF ** -0.5, 0.09375, ((0, 2), (1, 4), (2, 16))),
        "norm_bias": draw_norm_bias(jax.random.fold_in(splits[8], 71), 0),
    }


EPSILON = 1e-06
HIGHEST = lax.Precision.HIGHEST

@jax.custom_vjp
def low(v):
    return lax.optimization_barrier(v.astype(jnp.bfloat16)).astype(jnp.float32)

@jax.custom_vjp
def low_back(v):
    return v

def low_keep(v):
    return (low(v), None)

def low_pass(kept, grad):
    return (grad,)

def back_keep(v):
    return (v, None)

def back_low(kept, grad):
    return (low(grad),)
low.defvjp(low_keep, low_pass)
low_back.defvjp(back_keep, back_low)

def normalize(tok_rows, gain_row, shift_row):
    centred = tok_rows - lax.optimization_barrier(jnp.mean(tok_rows, axis=-1, keepdims=True))
    spread = lax.optimization_barrier(jnp.mean(centred * centred, axis=-1, keepdims=True))
    return centred * lax.rsqrt(spread + EPSILON) * gain_row + shift_row

def encoder_layer(weights, tok_rows):
    w_qkv, qv_bias, w_out, up_weight, up_bias, down_weight, vectors = weights
    image_count, seq_length, model_width = tok_rows.shape
    head_count = qv_bias.shape[1]
    head_width = qv_bias.shape[2]
    shape_heads = (image_count, seq_length, head_count, head_width)
    normed = low(normalize(tok_rows, vectors[0], vectors[1]))
    project = jnp.einsum('gld,dke->glke', normed, w_qkv, precision=HIGHEST)
    query = low(low_back((project[:, :, 0] + qv_bias[0].reshape(model_width)) * 0.125)).reshape(shape_heads)
    key_low = low(low_back(project[:, :, 1])).reshape(shape_heads)
    value_low = low(low_back(project[:, :, 2] + qv_bias[1].reshape(model_width))).reshape(shape_heads)
    scores = low_back(jnp.einsum('gqhe,gkhe->ghqk', query, key_low, precision=HIGHEST))
    probability = low(jax.nn.softmax(scores, axis=-1))
    attended = low(low_back(jnp.einsum('ghqk,gkhe->gqhe', probability, value_low, precision=HIGHEST)))
    attended = attended.reshape(image_count, seq_length, model_width)
    branch = low_back(jnp.einsum('gld,de->gle', attended, w_out, precision=HIGHEST))
    middle = tok_rows + branch + vectors[2]
    normed_two = low(normalize(middle, vectors[3], vectors[4]))
    hidden = low_back(jnp.einsum('gld,df->glf', normed_two, up_weight, precision=HIGHEST) + up_bias.reshape(-1))
    active = low(jax.nn.gelu(hidden, approximate=False))
    down_sum = low_back(jnp.einsum('glf,fd->gld', active, down_weight, precision=HIGHEST))
    return middle + down_sum + vectors[5]

def two_layers(weights, images_in):
    first_out = encoder_layer(jax.tree.map(lambda stacked: stacked[0], weights), images_in)
    passed = low(low_back(first_out))
    return encoder_layer(jax.tree.map(lambda stacked: stacked[1], weights), passed)

def reference(boundary, w_qkv, qv_bias, w_out, up_weight, up_bias, down_weight, norm_bias):
    weights = (w_qkv.astype(jnp.float32), qv_bias.astype(jnp.float32), w_out.astype(jnp.float32), up_weight.astype(jnp.float32), up_bias.astype(jnp.float32), down_weight.astype(jnp.float32), norm_bias.astype(jnp.float32))
    micro_count, image_count, seq_length, model_width = boundary.shape[1:]
    total_images = micro_count * image_count
    inputs = boundary[0].astype(jnp.float32).reshape(total_images, seq_length, model_width)
    cotangent = boundary[1].astype(jnp.float32).reshape(total_images, seq_length, model_width)
    group_size = 1
    for candidate in range(1, total_images + 1):
        if total_images % candidate == 0 and candidate * seq_length <= 4096:
            group_size = candidate

    def apply_all(params, flat_images):
        grouped = flat_images.reshape(total_images // group_size, group_size, seq_length, model_width)
        results = lax.map(jax.checkpoint(lambda images_in: two_layers(params, images_in)), grouped)
        return results.reshape(flat_images.shape)
    result, pullback = jax.vjp(apply_all, weights, inputs)
    grad_weights, grad_inputs = pullback(cotangent)
    whole_shape = (micro_count, image_count, seq_length, model_width)
    ends = jnp.stack([grad_inputs.reshape(whole_shape), result.reshape(whole_shape)])
    return (ends, grad_weights[0], grad_weights[1], grad_weights[2], grad_weights[3], grad_weights[4], grad_weights[5], grad_weights[6])
```

```python
from functools import partial
from types import SimpleNamespace
from typing import Any, NamedTuple

import jax
import jax.numpy as jnp
from jax import lax
from jax.experimental import pallas as pl
from jax.experimental.pallas import tpu as pltpu
from jax.sharding import Mesh
from jax.sharding import PartitionSpec as P

AXES = SECTION, DP_Y, DP_X, CORE, TENSOR = ("section", "dp_0", "dp_1", "dp_2", "tensor")
DP = (DP_Y, DP_X, CORE)
DP_TENSOR = (DP_Y, DP_X, CORE, TENSOR)
MESH = pl.DeviceIdType.MESH
BF, F32 = jnp.bfloat16, jnp.float32

X, Y, Z = "x", "y", "z"
SMALL, GRADS, TOTAL, PART, VEC, READY = "small", "grads", "total", "part", "vec", "ready"
EPSILON = 1e-06
T = 576
D = 1024
TILE = 144
N_TILES = T // TILE
SIZE = {Y: 4, X: 2, Z: 4}
NAME = {Y: DP_Y, X: DP_X, Z: TENSOR}

ORDERS = ((X, Y, Z), (X, Z, Y), (Y, Z, X), (Z, Y, X))
ROWS = ((48, 48, 16, 16), (48, 32, 32, 16), (32, 48, 16, 32))
MAX_ROWS = (48, 48, 32, 32)

NT = (((1,), (1,)), ((), ()))
TN = (((0,), (0,)), ((), ()))


def dot(a, b):
    return jnp.dot(a, b, preferred_element_type=F32)


def dot_nt(a, b):
    return lax.dot_general(a, b, NT, preferred_element_type=F32)


def dot_tn(a, b):
    return lax.dot_general(a, b, TN, preferred_element_type=F32)


class Step(NamedTuple):
    waits: list
    cost: float = 0.0
    sends: list = ()
    op: Any = None
    where: Any = None


RATE, LATENCY = 43500.0, 1.0


def in_order(chains, rate=RATE, latency=LATENCY):
    link_free = {}
    arrives = {}
    clock = 0.0
    place = [0] * len(chains)
    order = []
    while True:
        best = None
        for index, chain in enumerate(chains):
            if place[index] == len(chain):
                continue
            step = chain[place[index]]
            if any(task not in arrives for task in step.waits):
                continue
            ready = max([arrives[task] for task in step.waits], default=0.0)
            ready = max(ready, clock)
            if best is None or ready < best[0] - 1e-9:
                best = (ready, index)
        if best is None:
            assert all(p == len(c) for p, c in zip(place, chains))
            return order
        ready, index = best
        step = chains[index][place[index]]
        place[index] += 1
        clock = ready + step.cost
        for task, link, size in step.sends:
            if link is None:
                arrives[task] = clock
                continue
            begin = max(clock, link_free.get(link, 0.0))
            fast = 6.0 if link == CORE else 1.0
            link_free[link] = begin + size / rate / fast
            arrives[task] = link_free[link] + latency
            clock += 0.05
        order.append(step)


def note(*key):
    return (key, None, 0)


EDGE_TASKS = [((READY, 2), READY, 295000)]
CROSS_TASK = ((READY, 3), CORE, 590000)


def bytes_of(done, axis_fixed, rows, columns):
    blocks = 1
    for axis in done:
        blocks *= SIZE[axis]
    return blocks * rows * columns * 2


def gather_chain(group, order):
    rows = 8 if group == SMALL else ROWS[group][order]
    steps, waits, done = [], [], []
    for axis in ORDERS[order]:
        full = bytes_of(done, axis, rows, 512)
        key = (group, order, axis)
        if axis == X:
            steps.append(Step(waits, 0.0, [(key + ("s",), X, full)]))
            waits = [key + ("s",)]
        else:
            steps.append(Step(waits, 0.0, [(key + ("s+",), axis + "+", full), (key + ("s-",), axis + "-", full)]))
            steps.append(Step([key + ("s+",)], 0.0, [(key + ("f+",), axis + "+", full / 2)]))
            steps.append(Step([key + ("s-",)], 0.0, [(key + ("f-",), axis + "-", full / 2)]))
            waits = [key + ("f+",), key + ("f-",)]
        done.append(axis)
    steps.append(Step(waits, 0.0, [note(group, order)]))
    return steps


def reduce_chain(group, order, add):
    rows = ROWS[group][order]
    steps, end, cost = [], None, 0.0
    waits = [(GRADS, group)]
    left = list(ORDERS[order])
    per = 2e-6

    def step(waits, cost, op, sends):
        run = None if op is None else (lambda: add(group, order, op))
        steps.append(Step(waits, cost, sends, run))

    while left:
        axis = left.pop()
        full = bytes_of(left, axis, rows, 512)
        key = (GRADS, group, order, axis)
        if axis == X:
            step(waits, cost, end, [(key + ("s",), X, full)])
            waits = [key + ("s",)]
        else:
            step(waits, cost, end, [(key + ("h+",), axis + "+", full / 2), (key + ("h-",), axis + "-", full / 2)])
            step([key + ("h+",)], 0.2 + full / 4 * per, (axis, "h+"), [(key + ("s+",), axis + "+", full)])
            step([key + ("h-",)], 0.2 + full / 4 * per, (axis, "h-"), [(key + ("s-",), axis + "-", full)])
            waits = [key + ("s+",), key + ("s-",)]
        end = (axis, "end")
        cost = 0.2 + full * per
    step(waits, cost, end, [note(TOTAL, group, order)])
    return steps


GATHER_TASKS = {}
REDUCE_TASKS = {}
for _axes in ORDERS:
    for _axis in _axes:
        for _kind in ("s",) if _axis == X else ("s+", "s-", "f+", "f-"):
            GATHER_TASKS.setdefault((_axes, _axis, _kind), len(GATHER_TASKS))
        for _kind in ("s",) if _axis == X else ("s+", "s-", "h+", "h-"):
            REDUCE_TASKS.setdefault((_axes, _axis, _kind), len(REDUCE_TASKS))
N_TASKS = len(GATHER_TASKS)
N_SMALL = 9


def landing_shapes():
    shapes = {}
    for order, axes in enumerate(ORDERS):
        left = list(axes)
        while left:
            axis = left.pop()
            lead = tuple(SIZE[a] for a in (Z, Y, X) if a in left)
            for kind in ("s",) if axis == X else ("s+", "s-", "h+", "h-"):
                columns = 256 if kind[0] == "h" else 512
                shapes[(order, axis, kind)] = (3, *lead, MAX_ROWS[order], columns)
    return shapes


LANDINGS = landing_shapes()


def kernel(blocks_in, edge, small, out_rows, out_weights, out_vectors, *scratch):
    s = SimpleNamespace(**dict(zip(SCRATCH, scratch)))
    landing = dict(zip(LANDINGS, scratch[len(SCRATCH) :]))
    w, rows_in, h1, h2, qkv, o = s.w, s.rows_in, s.h1, s.h2, s.qkv, s.o
    r1, act, pull, probs = s.r1, s.act, s.pull, s.probs
    part, own, out_b, gr, do = s.part, s.own, s.out_b, s.gr, s.do
    tiles, norm_vec, qv_vec, up_vec = s.tiles, s.norm_vec, s.qv_vec, s.up_vec
    vec, vec_in, total = s.vec, s.vec_in, s.total

    sec = lax.axis_index(SECTION)
    y, x, core, z = (lax.axis_index(n) for n in (DP_Y, DP_X, CORE, TENSOR))
    here = {Y: y, X: x, Z: z}
    first = sec == 0

    def beside(axis, step):
        return lax.rem(here[axis] + step + SIZE[axis], SIZE[axis])

    def device(axis, step):
        return {NAME[axis]: beside(axis, step)}

    other_core = {CORE: 1 - core}
    other_section = {SECTION: 1 - sec}

    def send(src, dst, sems, where):
        return pltpu.make_async_remote_copy(
            src_ref=src, dst_ref=dst, send_sem=sems[0], recv_sem=sems[1], device_id=where, device_id_type=MESH
        )

    barrier = pltpu.get_barrier_semaphore()
    peers = [device(Y, 1), device(Y, 2), device(Y, 3), device(X, 1), other_section]
    peers += [device(Z, step) for step in (1, 2, 3)] + [other_core]
    peers += [{CORE: 1 - core, TENSOR: beside(Z, step)} for step in (1, 2, 3)]
    for peer in peers:
        pl.semaphore_signal(barrier, inc=1, device_id=peer, device_id_type=MESH)
    pl.semaphore_wait(barrier, len(peers))

    def own_rows(group):
        return w.at[group, z, y, x, pl.ds(pl.multiple_of(core * 64, 64), 64), :]

    local = [pltpu.make_async_copy(blocks_in.at[core, g], own_rows(g), s.local.at[g]) for g in range(3)]
    local.append(pltpu.make_async_copy(small, tiles.at[z, y, x, core], s.local.at[3]))
    swap = [
        send(blocks_in.at[1 - core, g], own_rows(g), (s.swap_s.at[g], s.swap_r.at[g]), other_core)
        for g in range(3)
    ]
    swap.append(send(small, tiles.at[z, y, x, core], (s.swap_s.at[3], s.swap_r.at[3]), other_core))
    for copy in swap + local:
        copy.start()

    def edge_copy(micro, half):
        to = 2 * micro + core
        src = edge.at[micro, :, pl.ds(half * 512, 512)]
        dst = rows_in.at[sec, pl.ds(pl.multiple_of(z * TILE, TILE), TILE), pl.ds(half * 512, 512)]
        stays = jnp.logical_and(to == z, core == half)
        where = {CORE: half, TENSOR: to}
        away = send(src, dst, (s.edge_s.at[micro, half], s.edge_r.at[z]), where)
        stay = pltpu.make_async_copy(src, dst, s.edge_r.at[z])
        return stays, away, stay

    def edge_start():
        for micro in range(2):
            for half in range(2):
                stays, away, stay = edge_copy(micro, half)

                @pl.when(stays)
                def _():
                    stay.start()

                @pl.when(jnp.logical_not(stays))
                def _():
                    away.start()

    half_image = rows_in.at[sec, :, pl.ds(pl.multiple_of(core * 512, 512), 512)]

    def cross():
        return send(half_image, half_image, (s.cross.at[0], s.cross.at[1]), other_core)

    def edge_arrived():
        for source in range(4):
            dst = rows_in.at[sec, pl.ds(source * TILE, TILE), pl.ds(pl.multiple_of(core * 512, 512), 512)]
            pltpu.make_async_copy(dst, dst, s.edge_r.at[source]).wait()
        cross().start()

    def edge_done():
        cross().wait()
        for micro in range(2):
            for half in range(2):
                stays, away, _ = edge_copy(micro, half)

                @pl.when(jnp.logical_not(stays))
                def _():
                    away.wait_send()

    for copy in local:
        copy.wait()
    for copy in swap:
        copy.wait()

    def region(group, at, row, rows, col, cols):
        index = [at[a] if at.get(a) is not None else slice(None) for a in (Z, Y, X)]
        return w.at[(group, *index, pl.ds(row, rows), pl.ds(col, cols))]

    def region_small(at, half):
        index = [at[a] if at.get(a) is not None else slice(None) for a in (Z, Y, X)]
        return tiles.at[(*index, slice(None) if half is None else half)]

    def gather_copy(task):
        group, order, axis, kind = task
        axes = ORDERS[order]
        done = axes[: axes.index(axis)]
        at = {a: here[a] for a in (Z, Y, X) if a not in done}
        step = -1 if kind.endswith("-") else 1
        half = None
        if kind[0] == "f":
            at[axis] = beside(axis, -step)
            half = 0 if step == 1 else 1
        sem = GATHER_TASKS[(axes, axis, kind)]
        if group == SMALL:
            ref = region_small(at, half)
            sems = (s.small_s.at[sem], s.small_r.at[sem])
        else:
            row = sum(ROWS[group][:order])
            col, cols = (0, 512) if half is None else (half * 256, 256)
            ref = region(group, at, row, ROWS[group][order], col, cols)
            sems = (s.link_s.at[group, sem], s.gather_r.at[group, sem])
        return send(ref, ref, sems, device(axis, step))

    def reduce_place(group, order, axis, at_axis, half):
        axes = ORDERS[order]
        later = axes[: axes.index(axis)]
        at = {a: here[a] for a in (Z, Y, X) if a not in later}
        at[axis] = at_axis
        row = sum(ROWS[group][:order])
        col, cols = (0, 512) if half is None else (half * 256, 256)
        return at, later, row, ROWS[group][order], col, cols

    def reduce_copy(task):
        _, group, order, axis, kind = task
        step = -1 if kind.endswith("-") else 1
        half = None
        if kind[0] == "h":
            half = 0 if step == 1 else 1
            at_axis = beside(axis, 2)
        else:
            at_axis = beside(axis, step)
        at, _, row, rows, col, cols = reduce_place(group, order, axis, at_axis, half)
        src = region(group, at, row, rows, col, cols)
        buffer = landing[(order, axis, kind)]
        lead = (slice(None),) * (len(buffer.shape) - 3)
        dst = buffer.at[(group, *lead, pl.ds(0, rows))]
        sem = REDUCE_TASKS[(ORDERS[order], axis, kind)]
        sems = (s.link_s.at[group, sem], s.reduce_r.at[group, sem])
        return send(src, dst, sems, device(axis, step))

    def part_copy(number, n):
        cols = pl.ds(n * 256 if isinstance(n, int) else pl.multiple_of(n * 256, 256), 256)
        sems = (s.part_s.at[number, n], s.part_r.at[number, n])
        return send(own.at[:, cols], part.at[number % 2, :, cols], sems, other_core)

    VEC_SLOT = {Y: 0, Z: 3, X: 6}

    def vec_copy(axis, step):
        slot = 7 if axis == CORE else VEC_SLOT[axis] + step - 1
        where = other_core if axis == CORE else device(axis, step)
        return send(vec, vec_in.at[slot], (s.vec_s.at[slot], s.vec_r.at[slot]), where)

    def copy_of(task):
        if task[0] == PART:
            return part_copy(*task[1:])
        if task[0] == VEC:
            return vec_copy(*task[1:])
        if task[0] == GRADS:
            return reduce_copy(task)
        return gather_copy(task)

    pending = []

    def emit(chains):
        links = {task for chain in chains for step in chain for task, link, _ in step.sends if link is not None}
        links -= {task for task, _, _ in EDGE_TASKS + [CROSS_TASK]}

        def run(step):
            for task in step.waits:
                if task in links:
                    copy_of(task).wait_recv()
            if step.op is not None:
                step.op()
            for task, link, _ in step.sends:
                if task in links:
                    if task[0] not in (PART, VEC):
                        pending.append(task)
                    copy_of(task).start()

        for step in in_order(chains):
            if step.where is None:
                run(step)
            else:
                pl.when(step.where)(lambda: run(step))

    def sent_all():
        for task in pending:
            copy_of(task).wait_send()
        pending.clear()

    def iota(shape, axis):
        return lax.broadcasted_iota(jnp.int32, shape, axis)

    def unpack(chunk):
        rows = tiles[chunk].reshape(256, 128)

        def spread(width, lane_of, dev_of, row_ok):
            lane = iota((128, width), 0)
            pick = (lane == lane_of(iota((128, width), 1))).astype(F32).astype(BF)
            wide = dot(rows, pick)
            i, n = iota((256, width), 0), iota((256, width), 1)
            keep = (i // 16 == dev_of(n)) & row_ok(i % 16, n)
            return jnp.where(keep, wide, 0.0).astype(BF)

        def fold(want, wide):
            a, i = iota((8, 256), 0), iota((8, 256), 1)
            return dot(want(a, i % 16).astype(F32).astype(BF), wide)

        wide = spread(
            1024,
            lambda n: n % 16,
            lambda n: jnp.where((n // 16) % 4 == chunk, n // 64, -1),
            lambda r, n: r < 6,
        )
        sums = fold(lambda a, r: a == r, wide)
        norm_vec[...] = sums if chunk == 0 else norm_vec[...] + sums
        wide = spread(
            128,
            lambda n: (2 * core + n // 64) * 4 + n % 4,
            lambda n: (n % 64) // 4,
            lambda r, n: (r == 6) | (r == 7),
        )
        both_rows = fold(lambda a, r: a == r - 6, wide)
        qv_vec[2 * chunk] = both_rows[0:1]
        qv_vec[2 * chunk + 1] = both_rows[1:2]
        wide = spread(
            512,
            lambda n: ((n // 64) % 4) * 4 + n % 4,
            lambda n: (n % 64) // 4,
            lambda r, n: r == 8 + 2 * core + n // 256,
        )
        one_row = fold(lambda a, r: (a == 0) & (r >= 0), wide)
        up_vec[2 * chunk] = one_row[0:1, :256]
        up_vec[2 * chunk + 1] = one_row[0:1, 256:]

    def vector(r):
        return norm_vec[r : r + 1, :]

    def span(i, size, align=None):
        if isinstance(i, int):
            return pl.ds(i * size, size)
        return pl.ds(pl.multiple_of(i * size, align or size), size)

    def tile(t):
        return span(t, TILE, 16)

    def both(number, rows):
        return own[rows, :].astype(F32) + part[number % 2, rows, :].astype(F32)

    def normed(value):
        centred = value - jnp.mean(value, axis=-1, keepdims=True)
        spread = jnp.mean(centred * centred, axis=-1, keepdims=True)
        scale = lax.rsqrt(spread + EPSILON)
        return centred * scale, scale

    def by_n(group, n, cut=slice(None)):
        return jnp.concatenate([w[group, g, n].reshape(256, 512)[:, cut] for g in range(4)], axis=1)

    def add_sum(row, value):
        s.sums[row] += value.reshape(value.shape[0] // 8, 8, D).sum(0)

    head_of = iota((1, 128), 1) // 64
    head_mask = [(head_of == j).astype(F32).astype(BF) for j in range(2)]

    def pick(a, b):
        return jnp.where(iota(a.shape, 1) < 64, a, b)

    def section_copy(slot, t, src):
        rows = tile(t)
        return send(src.at[rows], rows_in.at[slot, rows], (s.sec_s.at[t], s.sec_r.at[t]), other_section)

    def section_cross(slot, t):
        ref = rows_in.at[slot, tile(t)]
        return send(ref, ref, (s.sec_cross_s.at[t], s.sec_cross_r.at[t]), other_core)

    def section_pair(slot, k, use):
        mine, theirs = 2 * k + core, 2 * k + 1 - core
        section_copy(slot, mine, own).wait_recv()
        section_cross(slot, mine).start()
        use(mine)
        section_cross(slot, theirs).wait_recv()
        use(theirs)

    def section_forwarded(slot):
        for k in range(N_TILES // 2):
            section_cross(slot, 2 * k + core).wait_send()

    def section_send(slot, t, src):
        @pl.when(core == lax.rem(t, 2) if not isinstance(t, int) else core == t % 2)
        def _():
            section_copy(slot, t, src).start()

    def section_sent(slot, src):
        for k in range(N_TILES // 2):
            section_copy(slot, 2 * k + core, src).wait_send()

    def result_copy(src, owner):
        micro, owner_core = z // 2, lax.rem(z, 2)
        cols = pl.ds(pl.multiple_of(core * 512, 512), 512)
        from_ref = src.at[pl.ds(owner * TILE, TILE), cols]
        stays = jnp.logical_and(owner == z, core == owner_core)
        where = {CORE: owner_core, TENSOR: jnp.int32(owner)}
        to_ref = out_rows.at[micro, :, cols]
        sems = (s.res_s.at[owner], s.res_r.at[micro, core])
        return stays, send(from_ref, to_ref, sems, where), pltpu.make_async_copy(from_ref, to_ref, sems[1])

    def result_send(src):
        for owner in range(4):
            stays, away, stay = result_copy(src, owner)

            @pl.when(stays)
            def _():
                stay.start()

            @pl.when(jnp.logical_not(stays))
            def _():
                away.start()

    def result_sent(src):
        for owner in range(4):
            stays, away, stay = result_copy(src, owner)

            @pl.when(jnp.logical_not(stays))
            def _():
                away.wait_send()

    def norm_one(t):
        rows = tile(t)
        value, _ = normed(rows_in[0, rows, :].astype(F32))
        h1[rows, :] = (value * vector(0) + vector(1)).astype(BF)

    def project(pair):
        a, b = 2 * pair, 2 * pair + 1
        wa, wb = w[0, a].reshape(D, 512), w[0, b].reshape(D, 512)
        for half, weights in ((a, wa[:, :256]), (b, wb[:, :256])):
            p = dot(h1[...], weights)
            qkv[half, 0] = ((p[:, :128] + qv_vec[2 * half]) * 0.125).astype(BF)
            qkv[half, 1] = p[:, 128:].astype(BF)
        p = dot(h1[...], jnp.concatenate([wa[:, 256:384], wb[:, 256:384]], axis=1))
        qkv[a, 2] = (p[:, :128] + qv_vec[2 * a + 1]).astype(BF)
        qkv[b, 2] = (p[:, 128:] + qv_vec[2 * b + 1]).astype(BF)

    def attend(g):
        query, key, value = qkv[g, 0], qkv[g, 1], qkv[g, 2]
        outs = []
        for j in range(2):
            scores = dot_nt(key * head_mask[j], query)
            e = jnp.exp(scores - jnp.max(scores, axis=0, keepdims=True))
            p = (e * (1.0 / jnp.sum(e, axis=0, keepdims=True))).astype(BF)
            probs[2 * g + j] = p
            outs.append(dot_tn(p, value))
        o[:, span(g, 128)] = pick(*outs).astype(BF)

    def out_part(n):
        own[:, span(n, 256)] = dot_nt(o[...], by_n(0, n, slice(384, 512))).astype(BF)

    def norm_two(t):
        rows = tile(t)
        middle = rows_in[0, rows, :].astype(F32) + both(0, rows) + vector(2)
        r1[rows, :] = middle
        value, _ = normed(middle)
        h2[rows, :] = (value * vector(3) + vector(4)).astype(BF)

    def feed(i):
        g, half = (i // 2, i % 2) if isinstance(i, int) else (i // 2, lax.rem(i, 2))
        weights = w[1, g, :, :, :, span(half, 256)].reshape(D, 256)
        for t in range(2):
            rows = pl.ds(t * 288, 288)
            u = dot(h2[rows, :], weights) + up_vec[i]
            phi = 0.5 + 0.5 * lax.erf(u * (2.0**-0.5))
            act[rows, span(i, 256)] = (u * phi).astype(BF)
            pull[rows, span(i, 256)] = (phi + u * jnp.exp(u * u * -0.5) * 0.3989422804014327).astype(BF)

    def down(n):
        own[:, span(n, 256)] = dot_nt(act[...], by_n(2, n)).astype(BF)

    def finish(t):
        rows = tile(t)
        out_b[rows, :] = (r1[rows, :] + both(1, rows) + vector(5)).astype(BF)

    def feed_back(i):
        g, half = (i // 2, i % 2) if isinstance(i, int) else (i // 2, lax.rem(i, 2))
        ga = dot(rows_in[1], w[2, g, :, :, :, span(half, 256)].reshape(D, 256))
        du = (ga * pull[:, span(i, 256)].astype(F32)).astype(BF)
        pull[:, span(i, 256)] = du
        s.up_grad[i] = jnp.sum(du.astype(F32), axis=0, keepdims=True)

    def up_back(n):
        own[:, span(n, 256)] = dot_nt(pull[...], by_n(1, n)).astype(BF)

    def norm_back(value, grad, gain, gain_row, shift_row):
        hat, scale = normed(value)
        add_sum(gain_row, grad * hat)
        add_sum(shift_row, grad)
        dy = grad * gain
        return scale * (
            dy - jnp.mean(dy, axis=-1, keepdims=True) - hat * jnp.mean(dy * hat, axis=-1, keepdims=True)
        )

    def norm_two_back(t):
        rows = tile(t)
        pulled = norm_back(r1[rows, :], both(2, rows), vector(3), 3, 4)
        gy = rows_in[1, rows, :].astype(F32)
        grad = gy + pulled
        add_sum(5, gy)
        add_sum(2, grad)
        r1[rows, :] = grad
        gr[rows, :] = grad.astype(BF)

    def out_back(pair):
        weights = [w[0, 2 * pair + j, :, :, :, 384:512].reshape(D, 128) for j in range(2)]
        do[:, span(pair, 256)] = dot(gr[...], jnp.concatenate(weights, axis=1)).astype(BF)

    def attend_back(g):
        query, key, value = qkv[g, 0], qkv[g, 1], qkv[g, 2]
        grad = do[:, span(g, 128)]
        dq, dk, dv = [], [], []
        for j in range(2):
            p = probs[2 * g + j]
            dv.append(dot(p, grad))
            dp = dot_nt(value * head_mask[j], grad)
            p = p.astype(F32)
            ds = (p * (dp - jnp.sum(dp * p, axis=0, keepdims=True))).astype(BF)
            dk.append(dot(ds, query))
            dq.append(dot_tn(ds, key))
        dq, dk, dv = (pick(*pair).astype(BF) for pair in (dq, dk, dv))
        dq = dq * jnp.asarray(0.125, BF)
        qkv[g, 0] = dq
        qkv[g, 1] = dk
        qkv[g, 2] = dv
        s.qv_grad[2 * g] = jnp.sum(dq.astype(F32), axis=0, keepdims=True)
        s.qv_grad[2 * g + 1] = jnp.sum(dv.astype(F32), axis=0, keepdims=True)

    def qkv_all(first_g, last_g):
        return jnp.concatenate([qkv[g, k] for g in range(first_g, last_g) for k in range(3)], axis=1)

    def project_back(n):
        own[:, span(n, 256)] = dot_nt(qkv_all(0, 4), by_n(0, n, slice(0, 384))).astype(BF)

    def norm_one_back(t):
        rows = tile(t)
        pulled = norm_back(rows_in[0, rows, :].astype(F32), both(3, rows), vector(0), 0, 1)
        own[rows, :] = (r1[rows, :] + pulled).astype(BF)

    def zero_sums():
        s.sums[...] = jnp.zeros_like(s.sums)

    def fill_vec():
        vec[...] = jnp.zeros_like(vec)
        for r in range(6):
            vec[r : r + 1, :] = jnp.sum(s.sums[r], axis=0, keepdims=True)
        for r in range(8):
            vec[8 + r : 9 + r, 512:640] = s.qv_grad[r]
            vec[8 + r // 2 : 9 + r // 2, r % 2 * 256 : r % 2 * 256 + 256] = s.up_grad[r]

    def grads(group, m):
        def left(ref):
            return ref[:, m * 256 : m * 256 + 256].T

        def put(g, col, value):
            cols = value.shape[1]
            w[group, g, m, :, :, col : col + cols] = value.astype(BF).reshape(2, 128, cols)

        if group == 0:
            first_left, second_left = left(h1), left(gr)
            for pair in range(2):
                out = dot(first_left, qkv_all(2 * pair, 2 * pair + 2))
                put(2 * pair, 0, out[:, :384])
                put(2 * pair + 1, 0, out[:, 384:])
            out = dot(second_left, o[...])
            for g in range(4):
                put(g, 384, out[:, g * 128 : g * 128 + 128])
        else:
            rows, right = (h2, pull) if group == 1 else (rows_in.at[1], act)
            rows_t = left(rows)
            for g in range(4):
                put(g, 0, dot(rows_t, right[:, g * 512 : g * 512 + 512]))

    def exchanged(number):
        return [(PART, number, n) for n in range(4)]

    def part_steps(number, body, cost, waits):
        return [
            Step(waits if n == 0 else [], cost, [((PART, number, n), CORE, 295000)], partial(body, n))
            for n in range(4)
        ]

    def norm_steps(number, body, cost, after=None):
        def one(t):
            if t == 0:
                for n in range(4):
                    part_copy(number, n).wait_send()
            body(t)
            if after is not None:
                after(t)

        return [Step(exchanged(number) if t == 0 else [], cost, (), partial(one, t)) for t in range(N_TILES)]

    def everything(group):
        return [(group, order) for order in range(4)]

    forward = []
    forward += [Step([(READY, 1)] if t == 0 else [], 0.5, (), partial(norm_one, t)) for t in range(N_TILES)]
    forward += [Step(everything(0), 1.3, (), partial(project, p)) for p in range(2)]
    forward += [Step([], 1.6, (), partial(attend, g)) for g in range(4)]
    forward += part_steps(0, out_part, 0.4, [])
    forward += norm_steps(0, norm_two, 0.6)
    forward += [Step(everything(1), 0.6, (), partial(feed, i)) for i in range(8)]
    forward += part_steps(1, down, 0.8, everything(2))
    forward += norm_steps(1, finish, 0.3, lambda t: section_send(0, t, out_b))
    forward = [step._replace(where=first) for step in forward]
    unpacking = [Step([(SMALL, 0)], 1.5, (), partial(unpack, chunk)) for chunk in range(4)]
    edge_steps = [
        Step([], 0.2, EDGE_TASKS, edge_start),
        Step([(0, order) for order in range(4)], 0.2, [CROSS_TASK], edge_arrived),
        Step([CROSS_TASK[0]], 0.2, [note(READY, 1)], edge_done),
    ]
    gathers = [gather_chain(SMALL, 0)] + [gather_chain(g, o) for g in range(3) for o in range(4)]
    emit(gathers + [edge_steps, unpacking + forward])
    sent_all()

    def loop(count, body):
        def one(i, carry):
            body(i)
            return carry

        lax.fori_loop(0, count, one, 0)

    def exchange(number, body):
        def one(n):
            body(n)
            part_copy(number, n).start()

        loop(4, one)
        loop(4, lambda n: part_copy(number, n).wait())

    zero_sums()

    @pl.when(sec == 1)
    def _():
        for k in range(N_TILES // 2):
            section_pair(0, k, norm_one)
        loop(2, project)
        loop(4, attend)
        exchange(0, out_part)
        loop(4, norm_two)
        loop(8, feed)
        exchange(1, down)
        loop(4, finish)
        result_send(out_b)
        loop(8, feed_back)
        exchange(2, up_back)
        loop(4, norm_two_back)
        loop(2, out_back)
        loop(4, attend_back)
        exchange(3, project_back)

        def last(t):
            norm_one_back(t)
            section_send(1, t, own)

        loop(4, last)
        section_forwarded(0)

    def reduce_add(group, order, op):
        axis, kind = op
        if kind == "end":
            kinds = ("s",) if axis == X else ("s+", "s-")
            at_axis, half = here[axis], None
        else:
            kinds = (kind,)
            at_axis = beside(axis, 1 if kind == "h+" else -1)
            half = 0 if kind == "h+" else 1
        at, later, row, rows, col, cols = reduce_place(group, order, axis, at_axis, half)
        open_axes = [a for a in (Z, Y, X) if a in later]
        count = 1
        for a in open_axes:
            count *= SIZE[a]

        def one(i):
            rest, index = i, dict(at)
            for a in reversed(open_axes):
                index[a] = lax.rem(rest, SIZE[a])
                rest = rest // SIZE[a]
            lead = tuple(index[a] for a in open_axes)
            place = (group, index[Z], index[Y], index[X], pl.ds(row, rows), pl.ds(col, cols))
            value = w[place].astype(F32)
            for k in kinds:
                value += landing[(order, axis, k)][(group, *lead, pl.ds(0, rows), slice(None))].astype(F32)
            if later or kind != "end":
                w[place] = value.astype(BF)
            else:
                total[group, pl.ds(row, rows), :] = value

        if count == 1:
            one(0)
        else:
            loop(count, one)

    def vec_add(axis):
        value = vec[...]
        for step in range(1, SIZE[axis]):
            vec_copy(axis, step).wait_send()
            value += vec_in[VEC_SLOT[axis] + step - 1]
        vec[...] = value
        if axis == X:
            out_vectors[0] = value

    def vec_last():
        vec_copy(CORE, 1).wait_send()
        out_vectors[1] = vec_in[7]

    def vec_tasks(axis):
        return [((VEC, axis, step), VEC, 100000) for step in range(1, SIZE[axis])]

    def vec_waits(axis):
        return [(VEC, axis, step) for step in range(1, SIZE[axis])]

    vec_chain = [
        Step([(READY, 4)], 0.3, vec_tasks(Y), fill_vec),
        Step(vec_waits(Y), 0.2, vec_tasks(Z), lambda: vec_add(Y)),
        Step(vec_waits(Z), 0.2, vec_tasks(X), lambda: vec_add(Z)),
        Step(vec_waits(X), 0.2, [((VEC, CORE, 1), CORE, 65536)], lambda: vec_add(X)),
        Step([(VEC, CORE, 1)], 0.1, (), vec_last),
    ]

    def final_copy(group):
        src = total.at[group, pl.ds(pl.multiple_of((1 - core) * 64, 64), 64), :]
        return send(src, out_weights.at[group, core], (s.fin_s.at[group], s.fin_r.at[group]), other_core)

    def final_local(group):
        src = total.at[group, pl.ds(pl.multiple_of(core * 64, 64), 64), :]
        return pltpu.make_async_copy(src, out_weights.at[group, core], s.local.at[group])

    def final_start(group):
        final_copy(group).start()
        final_local(group).start()

    finals = [
        [Step([(TOTAL, group, order) for order in range(4)], 0.1, (), partial(final_start, group))]
        for group in (2, 1, 0)
    ]

    def receive_back():
        for k in range(N_TILES // 2):
            section_pair(1, k, lambda t: None)
        section_forwarded(1)

    def only_first(steps):
        return [step._replace(where=first) for step in steps]

    def grad_steps(group, cost):
        return [
            Step([], cost, [note(GRADS, group)] if m == 3 else (), partial(grads, group, m)) for m in range(4)
        ]

    backward = only_first([Step([], 0.0, (), receive_back)])
    backward += only_first([Step([], 0.35, (), partial(feed_back, i)) for i in range(8)])
    backward += grad_steps(2, 0.9)
    backward += only_first(part_steps(2, up_back, 0.8, []))
    backward += grad_steps(1, 1.0)
    backward += only_first(norm_steps(2, norm_two_back, 0.8))
    backward += only_first([Step([], 0.5, (), partial(out_back, p)) for p in range(2)])
    backward += only_first([Step([], 2.0, (), partial(attend_back, g)) for g in range(4)])
    backward += only_first(part_steps(3, project_back, 0.6, []))
    backward += grad_steps(0, 1.5)
    backward += only_first(norm_steps(3, norm_one_back, 0.8))
    backward += only_first([Step([], 0.1, (), lambda: result_send(own))])
    backward += [Step([], 0.0, [note(READY, 4)])]
    reduces = [reduce_chain(g, o, reduce_add) for g in (2, 1, 0) for o in range(4)]
    emit(reduces + finals + [vec_chain, backward])
    sent_all()

    for group in range(3):
        final_local(group).wait()
        final_copy(group).wait()

    @pl.when(first)
    def _():
        section_sent(0, out_b)
        result_sent(own)

    @pl.when(sec == 1)
    def _():
        section_sent(1, own)
        result_sent(out_b)

    for micro in range(2):
        for half in range(2):
            dst = out_rows.at[micro, :, pl.ds(half * 512, 512)]
            pltpu.make_async_copy(dst, dst, s.res_r.at[micro, half]).wait()


def dma(*shape):
    return pltpu.SemaphoreType.DMA(shape)


SCRATCH = dict(
    w=pltpu.VMEM((3, 4, 4, 2, 128, 512), BF),
    rows_in=pltpu.VMEM((2, T, D), BF),
    h1=pltpu.VMEM((T, D), BF),
    h2=pltpu.VMEM((T, D), BF),
    qkv=pltpu.VMEM((4, 3, T, 128), BF),
    o=pltpu.VMEM((T, 512), BF),
    r1=pltpu.VMEM((T, D), F32),
    act=pltpu.VMEM((T, 2048), BF),
    pull=pltpu.VMEM((T, 2048), BF),
    probs=pltpu.VMEM((8, T, T), BF),
    part=pltpu.VMEM((2, T, D), BF),
    own=pltpu.VMEM((T, D), BF),
    out_b=pltpu.VMEM((T, D), BF),
    gr=pltpu.VMEM((T, D), BF),
    do=pltpu.VMEM((T, 512), BF),
    tiles=pltpu.VMEM((4, 4, 2, 2, 16, 128), BF),
    norm_vec=pltpu.VMEM((8, D), F32),
    qv_vec=pltpu.VMEM((8, 1, 128), F32),
    up_vec=pltpu.VMEM((8, 1, 256), F32),
    sums=pltpu.VMEM((6, 8, D), F32),
    qv_grad=pltpu.VMEM((8, 1, 128), F32),
    up_grad=pltpu.VMEM((8, 1, 256), F32),
    vec=pltpu.VMEM((16, D), F32),
    vec_in=pltpu.VMEM((8, 16, D), F32),
    total=pltpu.VMEM((3, 128, 512), F32),
    local=dma(4),
    swap_s=dma(4),
    swap_r=dma(4),
    edge_s=dma(2, 2),
    edge_r=dma(4),
    cross=dma(2),
    small_s=dma(N_SMALL),
    small_r=dma(N_SMALL),
    link_s=dma(3, N_TASKS),
    gather_r=dma(3, N_TASKS),
    reduce_r=dma(3, N_TASKS),
    part_s=dma(4, N_TILES),
    part_r=dma(4, N_TILES),
    sec_s=dma(N_TILES),
    sec_r=dma(N_TILES),
    sec_cross_s=dma(N_TILES),
    sec_cross_r=dma(N_TILES),
    res_s=dma(4),
    res_r=dma(2, 2),
    vec_s=dma(8),
    vec_r=dma(8),
    fin_s=dma(3),
    fin_r=dma(3),
)


def run(blocks_in, edge, small):
    anywhere = pl.BlockSpec(memory_space=pl.ANY)
    vmem = pl.BlockSpec(memory_space=pltpu.VMEM)
    return pl.pallas_call(
        kernel,
        out_shape=(
            jax.ShapeDtypeStruct((2, TILE, D), BF),
            jax.ShapeDtypeStruct((3, 2, 64, 512), F32),
            jax.ShapeDtypeStruct((2, 16, D), F32),
        ),
        in_specs=[anywhere, anywhere, vmem],
        out_specs=(anywhere, anywhere, vmem),
        scratch_shapes=[*SCRATCH.values(), *(pltpu.VMEM(shape, BF) for shape in LANDINGS.values())],
        compiler_params=pltpu.CompilerParams(
            collective_id=0, has_side_effects=True, vmem_limit_bytes=62 << 20
        ),
    )(blocks_in, edge, small)


def body(boundary, w_qkv, qv_bias, w_out, up_weight, up_bias, down_weight, norm_bias):
    core, z = lax.axis_index(CORE), lax.axis_index(TENSOR)
    position = (lax.axis_index(DP_Y) * 2 + lax.axis_index(DP_X)) * 2 + core

    def halves(matrix):
        return jnp.moveaxis(matrix.reshape(64, 2, 512), 1, 0)

    attention = jnp.concatenate([w_qkv[0], w_out[0].T[:, None, :]], axis=1).reshape(64, 4, 2, 128)
    attention = jnp.moveaxis(attention, 2, 0).reshape(2, 64, 512)
    blocks_in = jnp.stack([attention, halves(up_weight[0]), halves(down_weight[0].T)], axis=1)
    small = jnp.concatenate([norm_bias[0], qv_bias[0].reshape(2, 16), up_bias[0].reshape(4, 16)])
    small = jnp.pad(small, ((0, 4), (0, 112)))

    out_rows, out_weights, out_vectors = run(blocks_in, boundary[0, :, 0], small)

    ends = out_rows.astype(F32)[None, :, None]
    attention = jnp.moveaxis(out_weights[0].reshape(2, 64, 4, 128), 0, 2).reshape(64, 4, 256)
    grad_up = jnp.moveaxis(out_weights[1], 0, 1).reshape(64, 1024)
    grad_down = jnp.moveaxis(out_weights[2], 0, 1).reshape(64, 1024).T
    norm_grad = lax.dynamic_slice(out_vectors[0], (0, (position * 4 + z) * 16), (6, 16))
    ordered = jnp.where(core == 0, out_vectors, out_vectors[::-1])
    qv = lax.dynamic_slice(ordered, (0, 8 + 2 * z, 512), (2, 2, 128)).reshape(2, 2, 2, 64)
    qv = jnp.moveaxis(qv, 0, 1).reshape(2, 4, 64)
    grad_qv = lax.dynamic_slice(qv, (0, 0, position * 4), (2, 4, 4))
    up = lax.dynamic_slice(ordered, (0, 8 + z, 0), (2, 1, 512)).reshape(16, 64)
    grad_up_bias = lax.dynamic_slice(up, (0, position * 4), (16, 4))
    return (
        ends,
        attention[None, :, :3],
        grad_qv[None],
        attention[:, 3].T[None],
        grad_up[None],
        grad_up_bias[None],
        grad_down[None],
        norm_grad[None],
    )


def solution(mesh):
    torus = Mesh(mesh.devices.reshape(mesh.shape[SECTION], 4, 2, 2, mesh.shape[TENSOR]), AXES)
    in_specs = (
        P(SECTION, None, DP, TENSOR, None),
        P(SECTION, DP, None, TENSOR),
        P(SECTION, None, TENSOR, DP),
        P(SECTION, TENSOR, DP),
        P(SECTION, DP, TENSOR),
        P(SECTION, TENSOR, DP),
        P(SECTION, TENSOR, DP),
        P(SECTION, None, DP_TENSOR),
    )
    return jax.shard_map(body, mesh=torus, in_specs=in_specs, out_specs=in_specs, check_vma=False)
```

```python
from functools import partial
from types import SimpleNamespace
from typing import Any, NamedTuple

import jax
import jax.numpy as jnp
from jax import lax
from jax.experimental import pallas as pl
from jax.experimental.pallas import tpu as pltpu
from jax.sharding import Mesh
from jax.sharding import PartitionSpec as P

AXES = SECTION, DP_Y, DP_X, CORE, TENSOR = ("section", "dp_0", "dp_1", "dp_2", "tensor")
DP = (DP_Y, DP_X, CORE)
DP_TENSOR = (DP_Y, DP_X, CORE, TENSOR)
MESH = pl.DeviceIdType.MESH
BF, F32 = jnp.bfloat16, jnp.float32

X, Y, Z = "x", "y", "z"
SMALL, GRADS, TOTAL, PART, VEC, READY = "small", "grads", "total", "part", "vec", "ready"
EPSILON = 1e-06
T = 576
D = 1024
TILE = 144
HALF = 288
N_TILES = T // TILE
SIZE = {Y: 4, X: 2, Z: 4}
NAME = {Y: DP_Y, X: DP_X, Z: TENSOR}

ORDERS = ((X, Y, Z), (X, Z, Y), (Y, Z, X), (Z, Y, X))
ROWS = ((48, 48, 16, 16), (48, 32, 32, 16), (32, 48, 16, 32))
MAX_ROWS = (48, 48, 32, 32)

NT = (((1,), (1,)), ((), ()))
TN = (((0,), (0,)), ((), ()))


def dot(a, b):
    return jnp.dot(a, b, preferred_element_type=F32)


def dot_nt(a, b):
    return lax.dot_general(a, b, NT, preferred_element_type=F32)


def dot_tn(a, b):
    return lax.dot_general(a, b, TN, preferred_element_type=F32)


class Step(NamedTuple):
    waits: list
    cost: float = 0.0
    sends: list = ()
    op: Any = None
    where: Any = None


RATE, LATENCY = 49000.0, 1.5


def in_order(chains, rate=RATE, latency=LATENCY):
    link_free = {}
    arrives = {}
    clock = 0.0
    place = [0] * len(chains)
    order = []
    while True:
        best = None
        for index, chain in enumerate(chains):
            if place[index] == len(chain):
                continue
            step = chain[place[index]]
            if any(task not in arrives for task in step.waits):
                continue
            ready = max([arrives[task] for task in step.waits], default=0.0)
            ready = max(ready, clock)
            if best is None or ready < best[0] - 1e-9:
                best = (ready, index)
        if best is None:
            assert all(p == len(c) for p, c in zip(place, chains))
            return order
        ready, index = best
        step = chains[index][place[index]]
        place[index] += 1
        clock = ready + step.cost
        for task, link, size in step.sends:
            if link is None:
                arrives[task] = clock
                continue
            begin = max(clock, link_free.get(link, 0.0))
            fast = 6.0 if link == CORE else 1.0
            link_free[link] = begin + size / rate / fast
            arrives[task] = link_free[link] + latency
            clock += 0.05
        order.append(step)


def note(*key):
    return (key, None, 0)


EDGE_TASKS = [((READY, 2), READY, 295000)]
CROSS_TASK = ((READY, 3), CORE, 590000)


def bytes_of(done, axis_fixed, rows, columns):
    blocks = 1
    for axis in done:
        blocks *= SIZE[axis]
    return blocks * rows * columns * 2


def gather_chain(group, order):
    rows = 8 if group == SMALL else ROWS[group][order]
    steps, waits, done = [], [], []
    for axis in ORDERS[order]:
        full = bytes_of(done, axis, rows, 512)
        key = (group, order, axis)
        if axis == X:
            steps.append(Step(waits, 0.0, [(key + ("s",), X, full)]))
            waits = [key + ("s",)]
        else:
            steps.append(Step(waits, 0.0, [(key + ("s+",), axis + "+", full), (key + ("s-",), axis + "-", full)]))
            steps.append(Step([key + ("s+",)], 0.0, [(key + ("f+",), axis + "+", full / 2)]))
            steps.append(Step([key + ("s-",)], 0.0, [(key + ("f-",), axis + "-", full / 2)]))
            waits = [key + ("f+",), key + ("f-",)]
        done.append(axis)
    if group != SMALL:
        last = next(i for i, step in enumerate(steps) if step.sends[0][0][2] == axis)
        if group:
            steps[last] = steps[last]._replace(waits=[*steps[last].waits, (READY, group - 1, order)])
        steps[-1].sends.append(note(READY, group, order))
    steps.append(Step(waits, 0.0, [note(group, order)]))
    return steps


def reduce_chain(group, order, add):
    rows = ROWS[group][order]
    steps, end, cost = [], None, 0.0
    waits = [(GRADS, group)]
    left = list(ORDERS[order])
    per = 0.6e-6

    def step(waits, cost, op, sends):
        run = None if op is None else (lambda: add(group, order, op))
        steps.append(Step(waits, cost, sends, run))

    while left:
        axis = left.pop()
        full = bytes_of(left, axis, rows, 512)
        key = (GRADS, group, order, axis)
        if axis == X:
            step(waits, cost, end, [(key + ("s",), X, full)])
            waits = [key + ("s",)]
        else:
            step(waits, cost, end, [(key + ("h+",), axis + "+", full / 2), (key + ("h-",), axis + "-", full / 2)])
            step([key + ("h+",)], 0.2 + full / 4 * per, (axis, "h+"), [(key + ("s+",), axis + "+", full)])
            step([key + ("h-",)], 0.2 + full / 4 * per, (axis, "h-"), [(key + ("s-",), axis + "-", full)])
            waits = [key + ("s+",), key + ("s-",)]
        end = (axis, "end")
        cost = 0.2 + full * per
    step(waits, cost, end, [note(TOTAL, group, order)])
    return steps


GATHER_TASKS = {}
REDUCE_TASKS = {}
for _axes in ORDERS:
    for _axis in _axes:
        for _kind in ("s",) if _axis == X else ("s+", "s-", "f+", "f-"):
            GATHER_TASKS.setdefault((_axes, _axis, _kind), len(GATHER_TASKS))
        for _kind in ("s",) if _axis == X else ("s+", "s-", "h+", "h-"):
            REDUCE_TASKS.setdefault((_axes, _axis, _kind), len(REDUCE_TASKS))
N_TASKS = len(GATHER_TASKS)
N_SMALL = 9


def landing_shapes():
    shapes = {}
    for order, axes in enumerate(ORDERS):
        left = list(axes)
        while left:
            axis = left.pop()
            lead = tuple(SIZE[a] for a in (Z, Y, X) if a in left)
            for kind in ("s",) if axis == X else ("s+", "s-", "h+", "h-"):
                columns = 256 if kind[0] == "h" else 512
                shapes[(order, axis, kind)] = (3, *lead, MAX_ROWS[order], columns)
    return shapes


LANDINGS = landing_shapes()


def kernel(edge, small, qkv_in, out_in, up_in, down_in, out_rows, out_weights, out_vectors, *scratch):
    s = SimpleNamespace(**dict(zip(SCRATCH, scratch)))
    landing = dict(zip(LANDINGS, scratch[len(SCRATCH) :]))
    w, rows_in, h1, h2, qkv, o = s.w, s.rows_in, s.h1, s.h2, s.qkv, s.o
    r1, act, pull, probs = s.r1, s.act, s.pull, s.probs
    part, own, out_b, gr, do = s.part, s.own, s.out_b, s.gr, s.do
    tiles, norm_vec, qv_vec, up_vec = s.tiles, s.norm_vec, s.qv_vec, s.up_vec
    vec, vec_in, total = s.vec, s.vec_in, s.total

    sec = lax.axis_index(SECTION)
    y, x, core, z = (lax.axis_index(n) for n in (DP_Y, DP_X, CORE, TENSOR))
    here = {Y: y, X: x, Z: z}
    first = sec == 0

    def beside(axis, step):
        return lax.rem(here[axis] + step + SIZE[axis], SIZE[axis])

    def device(axis, step):
        return {NAME[axis]: beside(axis, step)}

    other_core = {CORE: 1 - core}
    other_section = {SECTION: 1 - sec}

    def send(src, dst, sems, where):
        return pltpu.make_async_remote_copy(
            src_ref=src, dst_ref=dst, send_sem=sems[0], recv_sem=sems[1], device_id=where, device_id_type=MESH
        )

    barrier = pltpu.get_barrier_semaphore()
    peers = [device(Y, 1), device(Y, 2), device(Y, 3), device(X, 1), other_section]
    peers += [device(Z, step) for step in (1, 2, 3)] + [other_core]
    peers += [{CORE: 1 - core, TENSOR: beside(Z, step)} for step in (1, 2, 3)]
    for peer in peers:
        pl.semaphore_signal(barrier, inc=1, device_id=peer, device_id_type=MESH)
    blocks_in = s.blocks
    for half in range(2):
        narrow, wide = pl.ds(half * 128, 128), pl.ds(half * 512, 512)
        for k in range(3):
            blocks_in[half, 0, :, k * 128 : k * 128 + 128] = qkv_in[k, :, narrow]
        blocks_in[half, 0, :, 384:512] = out_in[:, narrow]
        blocks_in[half, 1] = up_in[:, wide]
        blocks_in[half, 2] = down_in[:, wide]
    pl.semaphore_wait(barrier, len(peers))

    def own_rows(group):
        return w.at[group, z, y, x, pl.ds(pl.multiple_of(core * 64, 64), 64), :]

    local = [pltpu.make_async_copy(blocks_in.at[core, g], own_rows(g), s.local.at[g]) for g in range(3)]
    local.append(pltpu.make_async_copy(small, tiles.at[z, y, x, core], s.local.at[3]))
    swap = [
        send(blocks_in.at[1 - core, g], own_rows(g), (s.swap_s.at[g], s.swap_r.at[g]), other_core)
        for g in range(3)
    ]
    swap.append(send(small, tiles.at[z, y, x, core], (s.swap_s.at[3], s.swap_r.at[3]), other_core))
    for copy in swap + local:
        copy.start()

    def edge_copy(micro, half):
        to = 2 * micro + core
        src = edge.at[micro, :, pl.ds(half * 512, 512)]
        dst = rows_in.at[sec, pl.ds(pl.multiple_of(z * TILE, TILE), TILE), pl.ds(half * 512, 512)]
        stays = jnp.logical_and(to == z, core == half)
        where = {CORE: half, TENSOR: to}
        away = send(src, dst, (s.edge_s.at[micro, half], s.edge_r.at[z]), where)
        stay = pltpu.make_async_copy(src, dst, s.edge_r.at[z])
        return stays, away, stay

    def edge_start():
        for micro in range(2):
            for half in range(2):
                stays, away, stay = edge_copy(micro, half)

                @pl.when(stays)
                def _():
                    stay.start()

                @pl.when(jnp.logical_not(stays))
                def _():
                    away.start()

    half_image = rows_in.at[sec, :, pl.ds(pl.multiple_of(core * 512, 512), 512)]

    def cross():
        return send(half_image, half_image, (s.cross.at[0], s.cross.at[1]), other_core)

    def edge_arrived():
        for source in range(4):
            dst = rows_in.at[sec, pl.ds(source * TILE, TILE), pl.ds(pl.multiple_of(core * 512, 512), 512)]
            pltpu.make_async_copy(dst, dst, s.edge_r.at[source]).wait()
        cross().start()

    def edge_done():
        cross().wait()
        for micro in range(2):
            for half in range(2):
                stays, away, _ = edge_copy(micro, half)

                @pl.when(jnp.logical_not(stays))
                def _():
                    away.wait_send()

    for copy in local:
        copy.wait()
    for copy in swap:
        copy.wait()

    def region(group, at, row, rows, col, cols):
        index = [at[a] if at.get(a) is not None else slice(None) for a in (Z, Y, X)]
        return w.at[(group, *index, pl.ds(row, rows), pl.ds(col, cols))]

    def region_small(at, half):
        index = [at[a] if at.get(a) is not None else slice(None) for a in (Z, Y, X)]
        return tiles.at[(*index, slice(None) if half is None else half)]

    def gather_copy(task):
        group, order, axis, kind = task
        axes = ORDERS[order]
        done = axes[: axes.index(axis)]
        at = {a: here[a] for a in (Z, Y, X) if a not in done}
        step = -1 if kind.endswith("-") else 1
        half = None
        if kind[0] == "f":
            at[axis] = beside(axis, -step)
            half = 0 if step == 1 else 1
        sem = GATHER_TASKS[(axes, axis, kind)]
        if group == SMALL:
            ref = region_small(at, half)
            sems = (s.small_s.at[sem], s.small_r.at[sem])
        else:
            row = sum(ROWS[group][:order])
            col, cols = (0, 512) if half is None else (half * 256, 256)
            ref = region(group, at, row, ROWS[group][order], col, cols)
            sems = (s.link_s.at[group, sem], s.gather_r.at[group, sem])
        return send(ref, ref, sems, device(axis, step))

    def reduce_place(group, order, axis, at_axis, half):
        axes = ORDERS[order]
        later = axes[: axes.index(axis)]
        at = {a: here[a] for a in (Z, Y, X) if a not in later}
        at[axis] = at_axis
        row = sum(ROWS[group][:order])
        col, cols = (0, 512) if half is None else (half * 256, 256)
        return at, later, row, ROWS[group][order], col, cols

    def reduce_copy(task):
        _, group, order, axis, kind = task
        step = -1 if kind.endswith("-") else 1
        half = None
        if kind[0] == "h":
            half = 0 if step == 1 else 1
            at_axis = beside(axis, 2)
        else:
            at_axis = beside(axis, step)
        at, _, row, rows, col, cols = reduce_place(group, order, axis, at_axis, half)
        src = region(group, at, row, rows, col, cols)
        buffer = landing[(order, axis, kind)]
        lead = (slice(None),) * (len(buffer.shape) - 3)
        dst = buffer.at[(group, *lead, pl.ds(0, rows))]
        sem = REDUCE_TASKS[(ORDERS[order], axis, kind)]
        sems = (s.link_s.at[group, sem], s.reduce_r.at[group, sem])
        return send(src, dst, sems, device(axis, step))

    def part_copy(number, n):
        sems = (s.part_s.at[number, n], s.part_r.at[number, n])
        if number % 2:
            return send(own.at[span(n, HALF, 16)], part.at[1, span(n, HALF, 16)], sems, other_core)
        cols = span(n, 256)
        return send(own.at[:, cols], part.at[0, :, cols], sems, other_core)

    VEC_SLOT = {Y: 0, Z: 3, X: 6}

    def vec_copy(axis, step):
        slot = 7 if axis == CORE else VEC_SLOT[axis] + step - 1
        where = other_core if axis == CORE else device(axis, step)
        return send(vec, vec_in.at[slot], (s.vec_s.at[slot], s.vec_r.at[slot]), where)

    def copy_of(task):
        if task[0] == PART:
            return part_copy(*task[1:])
        if task[0] == VEC:
            return vec_copy(*task[1:])
        if task[0] == GRADS:
            return reduce_copy(task)
        return gather_copy(task)

    pending = []

    def emit(chains, latency=LATENCY):
        links = {task for chain in chains for step in chain for task, link, _ in step.sends if link is not None}
        links -= {task for task, _, _ in EDGE_TASKS + [CROSS_TASK]}

        def run(step):
            for task in step.waits:
                if task in links:
                    copy_of(task).wait_recv()
            if step.op is not None:
                step.op()
            for task, link, _ in step.sends:
                if task in links:
                    if task[0] not in (PART, VEC):
                        pending.append(task)
                    copy_of(task).start()

        for step in in_order(chains, latency=latency):
            if step.where is None:
                run(step)
            else:
                pl.when(step.where)(lambda: run(step))

    def sent_all():
        for task in pending:
            copy_of(task).wait_send()
        pending.clear()

    def iota(shape, axis):
        return lax.broadcasted_iota(jnp.int32, shape, axis)

    def unpack(chunk):
        rows = tiles[chunk].reshape(256, 128)

        def spread(width, lane_of, dev_of, row_ok):
            lane = iota((128, width), 0)
            pick = (lane == lane_of(iota((128, width), 1))).astype(F32).astype(BF)
            wide = dot(rows, pick)
            i, n = iota((256, width), 0), iota((256, width), 1)
            keep = (i // 16 == dev_of(n)) & row_ok(i % 16, n)
            return jnp.where(keep, wide, 0.0).astype(BF)

        def fold(want, wide):
            a, i = iota((8, 256), 0), iota((8, 256), 1)
            return dot(want(a, i % 16).astype(F32).astype(BF), wide)

        wide = spread(
            1024,
            lambda n: n % 16,
            lambda n: jnp.where((n // 16) % 4 == chunk, n // 64, -1),
            lambda r, n: r < 6,
        )
        sums = fold(lambda a, r: a == r, wide)
        norm_vec[...] = sums if chunk == 0 else norm_vec[...] + sums
        wide = spread(
            128,
            lambda n: (2 * core + n // 64) * 4 + n % 4,
            lambda n: (n % 64) // 4,
            lambda r, n: (r == 6) | (r == 7),
        )
        both_rows = fold(lambda a, r: a == r - 6, wide)
        qv_vec[2 * chunk] = both_rows[0:1]
        qv_vec[2 * chunk + 1] = both_rows[1:2]
        wide = spread(
            512,
            lambda n: 8 * core + n // 64,
            lambda n: (n % 64) // 4,
            lambda r, n: r == 8 + n % 4,
        )
        one_row = fold(lambda a, r: (a == 0) & (r >= 0), wide)
        up_vec[2 * chunk] = one_row[0:1, :256]
        up_vec[2 * chunk + 1] = one_row[0:1, 256:]

    def vector(r):
        return norm_vec[r : r + 1, :]

    def span(i, size, align=None):
        if isinstance(i, int):
            return pl.ds(i * size, size)
        return pl.ds(pl.multiple_of(i * size, align or size), size)

    def tile(t):
        return span(t, TILE, 16)

    def both(number, rows):
        return own[rows, :].astype(F32) + part[number % 2, rows, :].astype(F32)

    def normed(value):
        centred = value - jnp.mean(value, axis=-1, keepdims=True)
        spread = jnp.mean(centred * centred, axis=-1, keepdims=True)
        scale = lax.rsqrt(spread + EPSILON)
        return centred * scale, scale

    def by_n(group, n, cut=slice(None)):
        return jnp.concatenate([w[group, g, n].reshape(256, 512)[:, cut] for g in range(4)], axis=1)

    def add_sum(row, value):
        s.sums[row] += value.reshape(value.shape[0] // 8, 8, D).sum(0)

    head_of = iota((1, 128), 1) // 64
    head_mask = [(head_of == j).astype(F32).astype(BF) for j in range(2)]

    def pick(a, b):
        return jnp.where(iota(a.shape, 1) < 64, a, b)

    def section_copy(slot, t, src):
        rows = tile(t)
        return send(src.at[rows], rows_in.at[slot, rows], (s.sec_s.at[t], s.sec_r.at[t]), other_section)

    def section_cross(slot, t):
        ref = rows_in.at[slot, tile(t)]
        return send(ref, ref, (s.sec_cross_s.at[t], s.sec_cross_r.at[t]), other_core)

    def section_pair(slot, k, use):
        mine, theirs = 2 * k + core, 2 * k + 1 - core
        section_copy(slot, mine, own).wait_recv()
        section_cross(slot, mine).start()
        use(mine)
        section_cross(slot, theirs).wait_recv()
        use(theirs)

    def section_forwarded(slot):
        for k in range(N_TILES // 2):
            section_cross(slot, 2 * k + core).wait_send()

    def section_send(slot, t, src):
        @pl.when(core == lax.rem(t, 2) if not isinstance(t, int) else core == t % 2)
        def _():
            section_copy(slot, t, src).start()

    def section_sent(slot, src):
        for k in range(N_TILES // 2):
            section_copy(slot, 2 * k + core, src).wait_send()

    def result_copy(src, owner):
        micro, owner_core = z // 2, lax.rem(z, 2)
        cols = pl.ds(pl.multiple_of(core * 512, 512), 512)
        from_ref = src.at[pl.ds(owner * TILE, TILE), cols]
        stays = jnp.logical_and(owner == z, core == owner_core)
        where = {CORE: owner_core, TENSOR: jnp.int32(owner)}
        to_ref = out_rows.at[micro, :, cols]
        sems = (s.res_s.at[owner], s.res_r.at[micro, core])
        return stays, send(from_ref, to_ref, sems, where), pltpu.make_async_copy(from_ref, to_ref, sems[1])

    def result_send(src):
        for owner in range(4):
            stays, away, stay = result_copy(src, owner)

            @pl.when(stays)
            def _():
                stay.start()

            @pl.when(jnp.logical_not(stays))
            def _():
                away.start()

    def result_sent(src):
        for owner in range(4):
            stays, away, stay = result_copy(src, owner)

            @pl.when(jnp.logical_not(stays))
            def _():
                away.wait_send()

    def norm_one(t):
        rows = tile(t)
        value, _ = normed(rows_in[0, rows, :].astype(F32))
        h1[rows, :] = (value * vector(0) + vector(1)).astype(BF)

    def project(pair, r):
        rows = span(r, HALF, 16)
        a, b = 2 * pair, 2 * pair + 1
        wa, wb = w[0, a].reshape(D, 512), w[0, b].reshape(D, 512)
        for half, weights in ((a, wa[:, :256]), (b, wb[:, :256])):
            p = dot(h1[rows, :], weights)
            qkv[half, 0, rows] = ((p[:, :128] + qv_vec[2 * half]) * 0.125).astype(BF)
            qkv[half, 1, rows] = p[:, 128:].astype(BF)
        p = dot(h1[rows, :], jnp.concatenate([wa[:, 256:384], wb[:, 256:384]], axis=1))
        qkv[a, 2, rows] = (p[:, :128] + qv_vec[2 * a + 1]).astype(BF)
        qkv[b, 2, rows] = (p[:, 128:] + qv_vec[2 * b + 1]).astype(BF)

    def attend(g):
        query, key, value = qkv[g, 0], qkv[g, 1], qkv[g, 2]
        outs = []
        for j in range(2):
            scores = dot_nt(key * head_mask[j], query)
            e = jnp.exp(scores - jnp.max(scores, axis=0, keepdims=True))
            p = (e * (1.0 / jnp.sum(e, axis=0, keepdims=True))).astype(BF)
            probs[2 * g + j] = p
            outs.append(dot_tn(p, value))
        o[:, span(g, 128)] = pick(*outs).astype(BF)

    def out_part(n):
        own[:, span(n, 256)] = dot_nt(o[...], by_n(0, n, slice(384, 512))).astype(BF)

    def norm_two(t):
        rows = tile(t)
        middle = rows_in[0, rows, :].astype(F32) + both(0, rows) + vector(2)
        r1[rows, :] = middle
        value, _ = normed(middle)
        h2[rows, :] = (value * vector(3) + vector(4)).astype(BF)

    def feed(i, with_grad=False):
        g, half = (i // 2, i % 2) if isinstance(i, int) else (i // 2, lax.rem(i, 2))
        weights = w[1, g, :, :, :, span(half, 256)].reshape(D, 256)
        for t in range(2):
            rows = pl.ds(t * 288, 288)
            u = dot(h2[rows, :], weights) + up_vec[i]
            phi = 0.5 + 0.5 * lax.erf(u * (2.0**-0.5))
            act[rows, span(i, 256)] = (u * phi).astype(BF)
            slope = phi + u * jnp.exp(u * u * -0.5) * 0.3989422804014327
            if with_grad:
                slope = slope * pull[rows, span(i, 256)].astype(F32)
            slope = slope.astype(BF)
            pull[rows, span(i, 256)] = slope
            if with_grad:
                add_bias(i, t, slope)

    def down(r, n):
        rows = span(r, HALF, 16)
        own[rows, span(n, 256)] = dot_nt(act[rows, :], by_n(2, n)).astype(BF)

    def finish(t):
        rows = tile(t)
        out_b[rows, :] = (r1[rows, :] + both(1, rows) + vector(5)).astype(BF)

    def add_bias(i, r, value):
        value = jnp.sum(value.astype(F32), axis=0, keepdims=True)
        s.up_grad[i] = value if r == 0 else s.up_grad[i] + value

    def feed_grad(i, rows):
        g, half = (i // 2, i % 2) if isinstance(i, int) else (i // 2, lax.rem(i, 2))
        return dot(rows_in[1, rows, :], w[2, g, :, :, :, span(half, 256)].reshape(D, 256))

    def feed_early(i):
        pull[:, span(i, 256)] = feed_grad(i, slice(None)).astype(BF)

    def feed_back(r, i):
        rows = pl.ds(r * HALF, HALF)
        du = (feed_grad(i, rows) * pull[rows, span(i, 256)].astype(F32)).astype(BF)
        pull[rows, span(i, 256)] = du
        add_bias(i, r, du)

    def up_back(n):
        own[:, span(n, 256)] = dot_nt(pull[...], by_n(1, n)).astype(BF)

    def norm_back(value, grad, gain, gain_row, shift_row):
        hat, scale = normed(value)
        add_sum(gain_row, grad * hat)
        add_sum(shift_row, grad)
        dy = grad * gain
        return scale * (
            dy - jnp.mean(dy, axis=-1, keepdims=True) - hat * jnp.mean(dy * hat, axis=-1, keepdims=True)
        )

    def norm_two_back(t):
        rows = tile(t)
        pulled = norm_back(r1[rows, :], both(2, rows), vector(3), 3, 4)
        gy = rows_in[1, rows, :].astype(F32)
        grad = gy + pulled
        add_sum(5, gy)
        add_sum(2, grad)
        r1[rows, :] = grad
        gr[rows, :] = grad.astype(BF)

    def out_back(pair):
        weights = [w[0, 2 * pair + j, :, :, :, 384:512].reshape(D, 128) for j in range(2)]
        do[:, span(pair, 256)] = dot(gr[...], jnp.concatenate(weights, axis=1)).astype(BF)

    def attend_back(g):
        query, key, value = qkv[g, 0], qkv[g, 1], qkv[g, 2]
        grad = do[:, span(g, 128)]
        dq, dk, dv = [], [], []
        for j in range(2):
            p = probs[2 * g + j]
            dv.append(dot(p, grad))
            dp = dot_nt(value * head_mask[j], grad)
            p = p.astype(F32)
            ds = (p * (dp - jnp.sum(dp * p, axis=0, keepdims=True))).astype(BF)
            dk.append(dot(ds, query))
            dq.append(dot_tn(ds, key))
        dq, dk, dv = (pick(*pair).astype(BF) for pair in (dq, dk, dv))
        dq = dq * jnp.asarray(0.125, BF)
        qkv[g, 0] = dq
        qkv[g, 1] = dk
        qkv[g, 2] = dv
        s.qv_grad[2 * g] = jnp.sum(dq.astype(F32), axis=0, keepdims=True)
        s.qv_grad[2 * g + 1] = jnp.sum(dv.astype(F32), axis=0, keepdims=True)

    def qkv_all(first_g, last_g, rows=slice(None)):
        return jnp.concatenate([qkv[g, k, rows] for g in range(first_g, last_g) for k in range(3)], axis=1)

    def project_back(r, n):
        rows = span(r, HALF, 16)
        own[rows, span(n, 256)] = dot_nt(qkv_all(0, 4, rows), by_n(0, n, slice(0, 384))).astype(BF)

    def norm_one_back(t):
        rows = tile(t)
        pulled = norm_back(rows_in[0, rows, :].astype(F32), both(3, rows), vector(0), 0, 1)
        own[rows, :] = (r1[rows, :] + pulled).astype(BF)

    def zero_sums():
        s.sums[...] = jnp.zeros_like(s.sums)

    def fill_vec():
        vec[...] = jnp.zeros_like(vec)
        for r in range(6):
            vec[r : r + 1, :] = jnp.sum(s.sums[r], axis=0, keepdims=True)
        for r in range(8):
            vec[8 + r : 9 + r, 512:640] = s.qv_grad[r]
            vec[8 + r // 2 : 9 + r // 2, r % 2 * 256 : r % 2 * 256 + 256] = s.up_grad[r]

    def grads(group, m):
        def left(ref):
            return ref[:, m * 256 : m * 256 + 256].T

        def put(g, col, value):
            cols = value.shape[1]
            w[group, g, m, :, :, col : col + cols] = value.astype(BF).reshape(2, 128, cols)

        if group == 0:
            first_left = left(h1)
            for pair in range(2):
                out = dot(first_left, qkv_all(2 * pair, 2 * pair + 2))
                put(2 * pair, 0, out[:, :384])
                put(2 * pair + 1, 0, out[:, 384:])
        else:
            rows, right = (h2, pull) if group == 1 else (rows_in.at[1], act)
            rows_t = left(rows)
            for g in range(4):
                put(g, 0, dot(rows_t, right[:, g * 512 : g * 512 + 512]))

    def out_grads(m):
        out = dot(gr[:, m * 256 : m * 256 + 256].T, o[...]).astype(BF)
        for g in range(4):
            w[0, g, m, :, :, 384:512] = out[:, g * 128 : g * 128 + 128].reshape(2, 128, 128)

    def part_steps(number, body, cost, waits):
        return [
            Step(waits if n == 0 else [], cost, [((PART, number, n), CORE, 295000)], partial(body, n))
            for n in range(4)
        ]

    def half_steps(number, body, cost, waits):
        return [
            Step(
                waits if (r, n) == (0, 0) else [],
                cost,
                [((PART, number, r), CORE, 590000)] if n == 3 else (),
                partial(body, r, n),
            )
            for r in range(2)
            for n in range(4)
        ]

    def norm_steps(number, body, cost, after=None):
        def one(t, pieces):
            for n in pieces:
                part_copy(number, n).wait_send()
            body(t)
            if after is not None:
                after(t)

        steps = []
        for t in range(N_TILES):
            if number % 2:
                pieces = [t // 2] if t % 2 == 0 else []
            else:
                pieces = list(range(4)) if t == 0 else []
            steps.append(Step([(PART, number, n) for n in pieces], cost, (), partial(one, t, pieces)))
        return steps

    def everything(group):
        return [(group, order) for order in range(4)]

    forward = []
    forward += [Step([(READY, 1)] if t == 0 else [], 0.5, (), partial(norm_one, t)) for t in range(N_TILES)]
    forward += [Step(everything(0), 0.7, (), partial(project, p, r)) for p in range(2) for r in range(2)]
    forward += [Step([], 1.6, (), partial(attend, g)) for g in range(4)]
    forward += part_steps(0, out_part, 0.4, [])
    forward += norm_steps(0, norm_two, 0.6)
    forward += [Step(everything(1), 0.6, (), partial(feed, i)) for i in range(8)]
    forward += half_steps(1, down, 0.5, everything(2))
    forward += norm_steps(1, finish, 0.3, lambda t: section_send(0, t, out_b))
    forward = [step._replace(where=first) for step in forward]
    unpacking = [Step([(SMALL, 0)], 1.5, (), partial(unpack, chunk)) for chunk in range(4)]
    edge_steps = [
        Step([], 0.2, EDGE_TASKS, edge_start),
        Step([(0, 3)], 0.2, [CROSS_TASK], edge_arrived),
        Step([CROSS_TASK[0]], 0.2, [note(READY, 1)], edge_done),
    ]
    gathers = [gather_chain(SMALL, 0)] + [gather_chain(g, o) for g in range(3) for o in range(4)]
    emit(gathers + [edge_steps, unpacking + forward])
    sent_all()

    def loop(count, body):
        def one(i, carry):
            body(i)
            return carry

        lax.fori_loop(0, count, one, 0)

    def exchange(number, body):
        def one(n):
            body(n)
            part_copy(number, n).start()

        loop(4, one)
        loop(4, lambda n: part_copy(number, n).wait())

    zero_sums()

    def exchange_halves(number, body, use):
        for r in range(2):
            loop(4, partial(body, r))
            part_copy(number, r).start()
        for r in range(2):
            part_copy(number, r).wait()
            loop(2, lambda t: use(2 * r + t))

    @pl.when(sec == 1)
    def _():
        loop(8, feed_early)
        for k in range(N_TILES // 2):
            section_pair(0, k, norm_one)
            loop(2, lambda pair: project(pair, k))
        loop(4, attend)
        exchange(0, out_part)
        loop(4, norm_two)
        loop(8, partial(feed, with_grad=True))
        exchange_halves(1, down, finish)
        result_send(out_b)
        exchange(2, up_back)
        loop(4, norm_two_back)
        loop(2, out_back)
        loop(4, attend_back)

        def last(t):
            norm_one_back(t)
            section_send(1, t, own)

        exchange_halves(3, project_back, last)
        section_forwarded(0)

    def reduce_add(group, order, op):
        axis, kind = op
        if kind == "end":
            kinds = ("s",) if axis == X else ("s+", "s-")
            at_axis, half = here[axis], None
        else:
            kinds = (kind,)
            at_axis = beside(axis, 1 if kind == "h+" else -1)
            half = 0 if kind == "h+" else 1
        at, later, row, rows, col, cols = reduce_place(group, order, axis, at_axis, half)
        open_axes = [a for a in (Z, Y, X) if a in later]
        count = 1
        for a in open_axes:
            count *= SIZE[a]

        def one(i):
            rest, index = i, dict(at)
            for a in reversed(open_axes):
                index[a] = lax.rem(rest, SIZE[a])
                rest = rest // SIZE[a]
            lead = tuple(index[a] for a in open_axes)
            place = (group, index[Z], index[Y], index[X], pl.ds(row, rows), pl.ds(col, cols))
            value = w[place].astype(F32)
            for k in kinds:
                value += landing[(order, axis, k)][(group, *lead, pl.ds(0, rows), slice(None))].astype(F32)
            if later or kind != "end":
                w[place] = value.astype(BF)
            else:
                total[group, pl.ds(row, rows), :] = value

        if count == 1:
            one(0)
        else:
            loop(count, one)

    def vec_add(axis):
        value = vec[...]
        for step in range(1, SIZE[axis]):
            vec_copy(axis, step).wait_send()
            value += vec_in[VEC_SLOT[axis] + step - 1]
        vec[...] = value
        if axis == X:
            out_vectors[0] = value

    def vec_last():
        vec_copy(CORE, 1).wait_send()
        out_vectors[1] = vec_in[7]

    def vec_tasks(axis):
        return [((VEC, axis, step), VEC, 100000) for step in range(1, SIZE[axis])]

    def vec_waits(axis):
        return [(VEC, axis, step) for step in range(1, SIZE[axis])]

    vec_chain = [
        Step([(READY, 4)], 0.3, vec_tasks(Y), fill_vec),
        Step(vec_waits(Y), 0.2, vec_tasks(Z), lambda: vec_add(Y)),
        Step(vec_waits(Z), 0.2, vec_tasks(X), lambda: vec_add(Z)),
        Step(vec_waits(X), 0.2, [((VEC, CORE, 1), CORE, 65536)], lambda: vec_add(X)),
        Step([(VEC, CORE, 1)], 0.1, (), vec_last),
    ]

    def final_copy(group):
        src = total.at[group, pl.ds(pl.multiple_of((1 - core) * 64, 64), 64), :]
        return send(src, out_weights.at[group, core], (s.fin_s.at[group], s.fin_r.at[group]), other_core)

    def final_local(group):
        src = total.at[group, pl.ds(pl.multiple_of(core * 64, 64), 64), :]
        return pltpu.make_async_copy(src, out_weights.at[group, core], s.local.at[group])

    def final_start(group):
        final_copy(group).start()
        final_local(group).start()

    finals = [
        [Step([(TOTAL, group, order) for order in range(4)], 0.1, (), partial(final_start, group))]
        for group in (2, 1, 0)
    ]

    def only_first(steps):
        return [step._replace(where=first) for step in steps]

    def grad_steps(group, cost):
        return [
            Step([], cost, [note(GRADS, group)] if m == 3 else (), partial(grads, group, m)) for m in range(4)
        ]

    backward = []
    for k in range(N_TILES // 2):
        backward += only_first([Step([], 0.0, (), partial(section_pair, 1, k, lambda t: None))])
        backward += only_first([Step([], 0.25, (), partial(feed_back, k, i)) for i in range(8)])
    backward += only_first([Step([], 0.0, (), partial(section_forwarded, 1))])
    backward += grad_steps(2, 0.9)
    backward += only_first(part_steps(2, up_back, 0.8, []))
    backward += grad_steps(1, 1.0)
    backward += only_first(norm_steps(2, norm_two_back, 0.8))
    backward += only_first([Step([], 0.5, (), partial(out_back, p)) for p in range(2)])
    backward += only_first([Step([], 2.0, (), partial(attend_back, g)) for g in range(4)])
    backward += only_first(half_steps(3, project_back, 0.35, []))
    backward += [Step([], 0.5, (), partial(out_grads, m)) for m in range(4)]
    backward += grad_steps(0, 1.0)
    backward += only_first(norm_steps(3, norm_one_back, 0.8))
    backward += only_first([Step([], 0.1, (), lambda: result_send(own))])
    backward += [Step([], 0.0, [note(READY, 4)])]
    reduces = [reduce_chain(g, o, reduce_add) for g in (2, 1, 0) for o in range(4)]
    emit(reduces + finals + [vec_chain, backward], latency=3.0)
    sent_all()

    for group in range(3):
        final_local(group).wait()
        final_copy(group).wait()

    @pl.when(first)
    def _():
        section_sent(0, out_b)
        result_sent(own)

    @pl.when(sec == 1)
    def _():
        section_sent(1, own)
        result_sent(out_b)

    for micro in range(2):
        for half in range(2):
            dst = out_rows.at[micro, :, pl.ds(half * 512, 512)]
            pltpu.make_async_copy(dst, dst, s.res_r.at[micro, half]).wait()


def dma(*shape):
    return pltpu.SemaphoreType.DMA(shape)


SCRATCH = dict(
    blocks=pltpu.VMEM((2, 3, 64, 512), BF),
    w=pltpu.VMEM((3, 4, 4, 2, 128, 512), BF),
    rows_in=pltpu.VMEM((2, T, D), BF),
    h1=pltpu.VMEM((T, D), BF),
    h2=pltpu.VMEM((T, D), BF),
    qkv=pltpu.VMEM((4, 3, T, 128), BF),
    o=pltpu.VMEM((T, 512), BF),
    r1=pltpu.VMEM((T, D), F32),
    act=pltpu.VMEM((T, 2048), BF),
    pull=pltpu.VMEM((T, 2048), BF),
    probs=pltpu.VMEM((8, T, T), BF),
    part=pltpu.VMEM((2, T, D), BF),
    own=pltpu.VMEM((T, D), BF),
    out_b=pltpu.VMEM((T, D), BF),
    gr=pltpu.VMEM((T, D), BF),
    do=pltpu.VMEM((T, 512), BF),
    tiles=pltpu.VMEM((4, 4, 2, 2, 16, 128), BF),
    norm_vec=pltpu.VMEM((8, D), F32),
    qv_vec=pltpu.VMEM((8, 1, 128), F32),
    up_vec=pltpu.VMEM((8, 1, 256), F32),
    sums=pltpu.VMEM((6, 8, D), F32),
    qv_grad=pltpu.VMEM((8, 1, 128), F32),
    up_grad=pltpu.VMEM((8, 1, 256), F32),
    vec=pltpu.VMEM((16, D), F32),
    vec_in=pltpu.VMEM((8, 16, D), F32),
    total=pltpu.VMEM((3, 128, 512), F32),
    local=dma(4),
    swap_s=dma(4),
    swap_r=dma(4),
    edge_s=dma(2, 2),
    edge_r=dma(4),
    cross=dma(2),
    small_s=dma(N_SMALL),
    small_r=dma(N_SMALL),
    link_s=dma(3, N_TASKS),
    gather_r=dma(3, N_TASKS),
    reduce_r=dma(3, N_TASKS),
    part_s=dma(4, N_TILES),
    part_r=dma(4, N_TILES),
    sec_s=dma(N_TILES),
    sec_r=dma(N_TILES),
    sec_cross_s=dma(N_TILES),
    sec_cross_r=dma(N_TILES),
    res_s=dma(4),
    res_r=dma(2, 2),
    vec_s=dma(8),
    vec_r=dma(8),
    fin_s=dma(3),
    fin_r=dma(3),
)


def finish_kernel(rows, weights, vectors, ends, qkv, qv, out, up, up_bias, down, norm):
    core, z = lax.axis_index(CORE), lax.axis_index(TENSOR)
    position = (lax.axis_index(DP_Y) * 2 + lax.axis_index(DP_X)) * 2 + core
    ends[...] = rows[...].astype(F32)
    for half in range(2):
        narrow, wide = slice(half * 128, half * 128 + 128), slice(half * 512, half * 512 + 512)
        for k in range(3):
            qkv[k, :, narrow] = weights[0, half, :, k * 128 : k * 128 + 128]
        out[:, narrow] = weights[0, half, :, 384:512]
        up[:, wide] = weights[1, half]
        down[:, wide] = weights[2, half]
    norm[...] = pltpu.roll(vectors[0], D - (position * 4 + z) * 16, 1)[:6, :16]
    for half in range(2):
        own = jnp.where(core == half, vectors[0], vectors[1])
        heads = pltpu.roll(pltpu.roll(own[8:16, 512:640], 128 - position * 4, 1), 8 - 2 * z, 0)
        hidden = pltpu.roll(pltpu.roll(own[8:16, :512], 512 - position * 4, 1), 8 - z, 0)
        for j in range(2):
            for part in range(2):
                qv[part, 2 * half + j : 2 * half + j + 1, :] = heads[part : part + 1, 64 * j : 64 * j + 4]
        for r in range(8):
            up_bias[8 * half + r : 8 * half + r + 1, :] = hidden[0:1, 64 * r : 64 * r + 4]


def body(boundary, w_qkv, qv_bias, w_out, up_weight, up_bias, down_weight, norm_bias):
    anywhere = pl.BlockSpec(memory_space=pl.ANY)
    vmem = pl.BlockSpec(memory_space=pltpu.VMEM)
    small = jnp.concatenate([norm_bias[0], qv_bias[0].reshape(2, 16), up_bias[0].T])
    small = jnp.pad(small, ((0, 4), (0, 112)))
    results = pl.pallas_call(
        kernel,
        out_shape=(
            jax.ShapeDtypeStruct((2, TILE, D), BF),
            jax.ShapeDtypeStruct((3, 2, 64, 512), F32),
            jax.ShapeDtypeStruct((2, 16, D), F32),
        ),
        in_specs=[anywhere] + [vmem] * 5,
        out_specs=(anywhere, anywhere, vmem),
        scratch_shapes=[*SCRATCH.values(), *(pltpu.VMEM(shape, BF) for shape in LANDINGS.values())],
        compiler_params=pltpu.CompilerParams(
            collective_id=0, has_side_effects=True, vmem_limit_bytes=62 << 20
        ),
    )(boundary[0, :, 0], small, jnp.moveaxis(w_qkv[0], 1, 0), w_out[0].T, up_weight[0], down_weight[0].T)
    shapes = ((2, TILE, D), (3, 64, 256), (2, 4, 4), (64, 256), (64, 1024), (16, 4), (64, 1024), (6, 16))
    ends, qkv, qv, out, up, up_bias_grad, down, norm = pl.pallas_call(
        finish_kernel,
        out_shape=tuple(jax.ShapeDtypeStruct(shape, F32) for shape in shapes),
        in_specs=[vmem] * 3,
        out_specs=(vmem,) * 8,
    )(*results)
    results = (jnp.moveaxis(qkv, 0, 1), qv, out.T, up, up_bias_grad, down.T, norm)
    return (ends[None, :, None], *(result[None] for result in results))


def solution(mesh):
    torus = Mesh(mesh.devices.reshape(mesh.shape[SECTION], 4, 2, 2, mesh.shape[TENSOR]), AXES)
    in_specs = (
        P(SECTION, None, DP, TENSOR, None),
        P(SECTION, DP, None, TENSOR),
        P(SECTION, None, TENSOR, DP),
        P(SECTION, TENSOR, DP),
        P(SECTION, DP, TENSOR),
        P(SECTION, TENSOR, DP),
        P(SECTION, TENSOR, DP),
        P(SECTION, None, DP_TENSOR),
    )
    return jax.shard_map(body, mesh=torus, in_specs=in_specs, out_specs=in_specs, check_vma=False)
```

```python
from functools import partial
from types import SimpleNamespace
from typing import Any, NamedTuple

import jax
import jax.numpy as jnp
from jax import lax
from jax.experimental import pallas as pl
from jax.experimental.pallas import tpu as pltpu
from jax.sharding import Mesh
from jax.sharding import PartitionSpec as P

AXES = SECTION, DP_Y, DP_X, CORE, TENSOR = ("section", "dp_0", "dp_1", "dp_2", "tensor")
DP = (DP_Y, DP_X, CORE)
DP_TENSOR = (DP_Y, DP_X, CORE, TENSOR)
MESH = pl.DeviceIdType.MESH
BF, F32 = jnp.bfloat16, jnp.float32

X, Y, Z = "x", "y", "z"
SMALL, GRADS, TOTAL, PART, VEC, READY = "small", "grads", "total", "part", "vec", "ready"
EPSILON = 1e-06
T = 576
D = 1024
TILE = 144
HALF = 288
N_TILES = T // TILE
SIZE = {Y: 4, X: 2, Z: 4}
NAME = {Y: DP_Y, X: DP_X, Z: TENSOR}

ORDERS = ((X, Y, Z), (X, Z, Y), (Y, Z, X), (Z, Y, X))
ROWS = ((48, 48, 16, 16), (48, 32, 32, 16), (32, 48, 16, 32))
MAX_ROWS = (48, 48, 32, 32)

NT = (((1,), (1,)), ((), ()))
TN = (((0,), (0,)), ((), ()))


def dot(a, b):
    return jnp.dot(a, b, preferred_element_type=F32)


def dot_nt(a, b):
    return lax.dot_general(a, b, NT, preferred_element_type=F32)


def dot_tn(a, b):
    return lax.dot_general(a, b, TN, preferred_element_type=F32)


class Step(NamedTuple):
    waits: list
    cost: float = 0.0
    sends: list = ()
    op: Any = None
    where: Any = None


RATE, LATENCY = 49000.0, 1.5


def in_order(chains, rate=RATE, latency=LATENCY):
    link_free = {}
    arrives = {}
    clock = 0.0
    place = [0] * len(chains)
    order = []
    while True:
        best = None
        for index, chain in enumerate(chains):
            if place[index] == len(chain):
                continue
            step = chain[place[index]]
            if any(task not in arrives for task in step.waits):
                continue
            ready = max([arrives[task] for task in step.waits], default=0.0)
            ready = max(ready, clock)
            if best is None or ready < best[0] - 1e-9:
                best = (ready, index)
        if best is None:
            assert all(p == len(c) for p, c in zip(place, chains))
            return order
        ready, index = best
        step = chains[index][place[index]]
        place[index] += 1
        clock = ready + step.cost
        for task, link, size in step.sends:
            if link is None:
                arrives[task] = clock
                continue
            begin = max(clock, link_free.get(link, 0.0))
            fast = 6.0 if link == CORE else 1.0
            link_free[link] = begin + size / rate / fast
            arrives[task] = link_free[link] + latency
            clock += 0.05
        order.append(step)


def note(*key):
    return (key, None, 0)


EDGE_TASKS = [((READY, 2), READY, 295000)]
CROSS_TASK = ((READY, 3), CORE, 590000)


def bytes_of(done, axis_fixed, rows, columns):
    blocks = 1
    for axis in done:
        blocks *= SIZE[axis]
    return blocks * rows * columns * 2


def gather_chain(group, order):
    rows = 8 if group == SMALL else ROWS[group][order]
    steps, waits, done = [], [], []
    for axis in ORDERS[order]:
        full = bytes_of(done, axis, rows, 512)
        key = (group, order, axis)
        if axis == X:
            steps.append(Step(waits, 0.0, [(key + ("s",), X, full)]))
            waits = [key + ("s",)]
        else:
            steps.append(Step(waits, 0.0, [(key + ("s+",), axis + "+", full), (key + ("s-",), axis + "-", full)]))
            steps.append(Step([key + ("s+",)], 0.0, [(key + ("f+",), axis + "+", full / 2)]))
            steps.append(Step([key + ("s-",)], 0.0, [(key + ("f-",), axis + "-", full / 2)]))
            waits = [key + ("f+",), key + ("f-",)]
        done.append(axis)
    if group != SMALL:
        last = next(i for i, step in enumerate(steps) if step.sends[0][0][2] == axis)
        if group:
            steps[last] = steps[last]._replace(waits=[*steps[last].waits, (READY, 0, order)])
        steps[-1].sends.append(note(READY, group, order))
    steps.append(Step(waits, 0.0, [note(group, order)]))
    return steps


def reduce_chain(group, order, add):
    rows = ROWS[group][order]
    steps, end, cost = [], None, 0.0
    waits = [(GRADS, group)]
    left = list(ORDERS[order])
    per = 0.3e-6

    def step(waits, cost, op, sends):
        run = None if op is None else (lambda: add(group, order, op))
        steps.append(Step(waits, cost, sends, run))

    while left:
        axis = left.pop()
        full = bytes_of(left, axis, rows, 512)
        key = (GRADS, group, order, axis)
        if axis == X:
            step(waits, cost, end, [(key + ("s",), X, full)])
            waits = [key + ("s",)]
        else:
            step(waits, cost, end, [(key + ("h+",), axis + "+", full / 2), (key + ("h-",), axis + "-", full / 2)])
            step([key + ("h+",)], 0.1 + full / 4 * per, (axis, "h+"), [(key + ("s+",), axis + "+", full)])
            step([key + ("h-",)], 0.1 + full / 4 * per, (axis, "h-"), [(key + ("s-",), axis + "-", full)])
            waits = [key + ("s+",), key + ("s-",)]
        end = (axis, "end")
        cost = 0.1 + full * per
    step(waits, cost, end, [note(TOTAL, group, order)])
    return steps


GATHER_TASKS = {}
REDUCE_TASKS = {}
for _axes in ORDERS:
    for _axis in _axes:
        for _kind in ("s",) if _axis == X else ("s+", "s-", "f+", "f-"):
            GATHER_TASKS.setdefault((_axes, _axis, _kind), len(GATHER_TASKS))
        for _kind in ("s",) if _axis == X else ("s+", "s-", "h+", "h-"):
            REDUCE_TASKS.setdefault((_axes, _axis, _kind), len(REDUCE_TASKS))
N_TASKS = len(GATHER_TASKS)
N_SMALL = 9


def landing_shapes():
    shapes = {}
    for order, axes in enumerate(ORDERS):
        left = list(axes)
        while left:
            axis = left.pop()
            lead = tuple(SIZE[a] for a in (Z, Y, X) if a in left)
            for kind in ("s",) if axis == X else ("s+", "s-", "h+", "h-"):
                columns = 256 if kind[0] == "h" else 512
                shapes[(order, axis, kind)] = (3, *lead, MAX_ROWS[order], columns)
    return shapes


LANDINGS = landing_shapes()


def kernel(edge, small, qkv_in, out_in, up_in, down_in, out_rows, out_weights, out_vectors, *scratch):
    s = SimpleNamespace(**dict(zip(SCRATCH, scratch)))
    landing = dict(zip(LANDINGS, scratch[len(SCRATCH) :]))
    w, rows_in, h1, h2, qkv, o = s.w, s.rows_in, s.h1, s.h2, s.qkv, s.o
    r1, act, pull, probs = s.r1, s.act, s.pull, s.probs
    part, own, out_b, gr, do = s.part, s.own, s.out_b, s.gr, s.do
    tiles, norm_vec, qv_vec, up_vec = s.tiles, s.norm_vec, s.qv_vec, s.up_vec
    vec, vec_in, total = s.vec, s.vec_in, s.total

    sec = lax.axis_index(SECTION)
    y, x, core, z = (lax.axis_index(n) for n in (DP_Y, DP_X, CORE, TENSOR))
    here = {Y: y, X: x, Z: z}
    first = sec == 0

    def beside(axis, step):
        return lax.rem(here[axis] + step + SIZE[axis], SIZE[axis])

    def device(axis, step):
        return {NAME[axis]: beside(axis, step)}

    other_core = {CORE: 1 - core}
    other_section = {SECTION: 1 - sec}

    def send(src, dst, sems, where):
        return pltpu.make_async_remote_copy(
            src_ref=src, dst_ref=dst, send_sem=sems[0], recv_sem=sems[1], device_id=where, device_id_type=MESH
        )

    barrier = pltpu.get_barrier_semaphore()
    peers = [device(Y, 1), device(Y, 2), device(Y, 3), device(X, 1), other_section]
    peers += [device(Z, step) for step in (1, 2, 3)] + [other_core]
    peers += [{CORE: 1 - core, TENSOR: beside(Z, step)} for step in (1, 2, 3)]
    for peer in peers:
        pl.semaphore_signal(barrier, inc=1, device_id=peer, device_id_type=MESH)
    blocks_in = s.blocks
    for half in range(2):
        narrow, wide = pl.ds(half * 128, 128), pl.ds(half * 512, 512)
        for k in range(3):
            blocks_in[half, 0, :, k * 128 : k * 128 + 128] = qkv_in[k, :, narrow]
        blocks_in[half, 0, :, 384:512] = out_in[:, narrow]
        blocks_in[half, 1] = up_in[:, wide]
        blocks_in[half, 2] = down_in[:, wide]
    pl.semaphore_wait(barrier, len(peers))

    def own_rows(group):
        return w.at[group, z, y, x, pl.ds(pl.multiple_of(core * 64, 64), 64), :]

    local = [pltpu.make_async_copy(blocks_in.at[core, g], own_rows(g), s.local.at[g]) for g in range(3)]
    local.append(pltpu.make_async_copy(small, tiles.at[z, y, x, core], s.local.at[3]))
    swap = [
        send(blocks_in.at[1 - core, g], own_rows(g), (s.swap_s.at[g], s.swap_r.at[g]), other_core)
        for g in range(3)
    ]
    swap.append(send(small, tiles.at[z, y, x, core], (s.swap_s.at[3], s.swap_r.at[3]), other_core))
    for copy in swap + local:
        copy.start()

    def edge_copy(micro, half):
        to = 2 * micro + core
        src = edge.at[micro, :, pl.ds(half * 512, 512)]
        dst = rows_in.at[sec, pl.ds(pl.multiple_of(z * TILE, TILE), TILE), pl.ds(half * 512, 512)]
        stays = jnp.logical_and(to == z, core == half)
        where = {CORE: half, TENSOR: to}
        away = send(src, dst, (s.edge_s.at[micro, half], s.edge_r.at[z]), where)
        stay = pltpu.make_async_copy(src, dst, s.edge_r.at[z])
        return stays, away, stay

    def edge_start():
        for micro in range(2):
            for half in range(2):
                stays, away, stay = edge_copy(micro, half)

                @pl.when(stays)
                def _():
                    stay.start()

                @pl.when(jnp.logical_not(stays))
                def _():
                    away.start()

    half_image = rows_in.at[sec, :, pl.ds(pl.multiple_of(core * 512, 512), 512)]

    def cross():
        return send(half_image, half_image, (s.cross.at[0], s.cross.at[1]), other_core)

    def edge_arrived():
        for source in range(4):
            dst = rows_in.at[sec, pl.ds(source * TILE, TILE), pl.ds(pl.multiple_of(core * 512, 512), 512)]
            pltpu.make_async_copy(dst, dst, s.edge_r.at[source]).wait()
        cross().start()

    def edge_done():
        cross().wait()
        for micro in range(2):
            for half in range(2):
                stays, away, _ = edge_copy(micro, half)

                @pl.when(jnp.logical_not(stays))
                def _():
                    away.wait_send()

    for copy in local:
        copy.wait()
    for copy in swap:
        copy.wait()

    def region(group, at, row, rows, col, cols):
        index = [at[a] if at.get(a) is not None else slice(None) for a in (Z, Y, X)]
        return w.at[(group, *index, pl.ds(row, rows), pl.ds(col, cols))]

    def region_small(at, half):
        index = [at[a] if at.get(a) is not None else slice(None) for a in (Z, Y, X)]
        return tiles.at[(*index, slice(None) if half is None else half)]

    def gather_copy(task):
        group, order, axis, kind = task
        axes = ORDERS[order]
        done = axes[: axes.index(axis)]
        at = {a: here[a] for a in (Z, Y, X) if a not in done}
        step = -1 if kind.endswith("-") else 1
        half = None
        if kind[0] == "f":
            at[axis] = beside(axis, -step)
            half = 0 if step == 1 else 1
        sem = GATHER_TASKS[(axes, axis, kind)]
        if group == SMALL:
            ref = region_small(at, half)
            sems = (s.small_s.at[sem], s.small_r.at[sem])
        else:
            row = sum(ROWS[group][:order])
            col, cols = (0, 512) if half is None else (half * 256, 256)
            ref = region(group, at, row, ROWS[group][order], col, cols)
            sems = (s.link_s.at[group, sem], s.gather_r.at[group, sem])
        return send(ref, ref, sems, device(axis, step))

    def reduce_place(group, order, axis, at_axis, half):
        axes = ORDERS[order]
        later = axes[: axes.index(axis)]
        at = {a: here[a] for a in (Z, Y, X) if a not in later}
        at[axis] = at_axis
        row = sum(ROWS[group][:order])
        col, cols = (0, 512) if half is None else (half * 256, 256)
        return at, later, row, ROWS[group][order], col, cols

    def reduce_copy(task):
        _, group, order, axis, kind = task
        step = -1 if kind.endswith("-") else 1
        half = None
        if kind[0] == "h":
            half = 0 if step == 1 else 1
            at_axis = beside(axis, 2)
        else:
            at_axis = beside(axis, step)
        at, _, row, rows, col, cols = reduce_place(group, order, axis, at_axis, half)
        src = region(group, at, row, rows, col, cols)
        buffer = landing[(order, axis, kind)]
        lead = (slice(None),) * (len(buffer.shape) - 3)
        dst = buffer.at[(group, *lead, pl.ds(0, rows))]
        sem = REDUCE_TASKS[(ORDERS[order], axis, kind)]
        sems = (s.link_s.at[group, sem], s.reduce_r.at[group, sem])
        return send(src, dst, sems, device(axis, step))

    def part_copy(number, n):
        sems = (s.part_s.at[number, n], s.part_r.at[number, n])
        if number % 2:
            return send(own.at[span(n, HALF, 16)], part.at[1, span(n, HALF, 16)], sems, other_core)
        cols = span(n, 256)
        return send(own.at[:, cols], part.at[0, :, cols], sems, other_core)

    VEC_SLOT = {Y: 0, Z: 3, X: 6}

    def vec_copy(axis, step):
        slot = 7 if axis == CORE else VEC_SLOT[axis] + step - 1
        where = other_core if axis == CORE else device(axis, step)
        return send(vec, vec_in.at[slot], (s.vec_s.at[slot], s.vec_r.at[slot]), where)

    def copy_of(task):
        if task[0] == PART:
            return part_copy(*task[1:])
        if task[0] == VEC:
            return vec_copy(*task[1:])
        if task[0] == GRADS:
            return reduce_copy(task)
        return gather_copy(task)

    pending = []

    def emit(chains, latency=LATENCY):
        links = {task for chain in chains for step in chain for task, link, _ in step.sends if link is not None}
        links -= {task for task, _, _ in EDGE_TASKS + [CROSS_TASK]}

        def run(step):
            for task in step.waits:
                if task in links:
                    copy_of(task).wait_recv()
            if step.op is not None:
                step.op()
            for task, link, _ in step.sends:
                if task in links:
                    if task[0] not in (PART, VEC):
                        pending.append(task)
                    copy_of(task).start()

        for step in in_order(chains, latency=latency):
            if step.where is None:
                run(step)
            else:
                pl.when(step.where)(lambda: run(step))

    def sent_all():
        for task in pending:
            copy_of(task).wait_send()
        pending.clear()

    def iota(shape, axis):
        return lax.broadcasted_iota(jnp.int32, shape, axis)

    def unpack(chunk):
        rows = tiles[chunk].reshape(256, 128)

        def spread(width, lane_of, dev_of, row_ok):
            lane = iota((128, width), 0)
            pick = (lane == lane_of(iota((128, width), 1))).astype(F32).astype(BF)
            wide = dot(rows, pick)
            i, n = iota((256, width), 0), iota((256, width), 1)
            keep = (i // 16 == dev_of(n)) & row_ok(i % 16, n)
            return jnp.where(keep, wide, 0.0).astype(BF)

        def fold(want, wide):
            a, i = iota((8, 256), 0), iota((8, 256), 1)
            return dot(want(a, i % 16).astype(F32).astype(BF), wide)

        wide = spread(
            1024,
            lambda n: n % 16,
            lambda n: jnp.where((n // 16) % 4 == chunk, n // 64, -1),
            lambda r, n: r < 6,
        )
        sums = fold(lambda a, r: a == r, wide)
        norm_vec[...] = sums if chunk == 0 else norm_vec[...] + sums
        wide = spread(
            128,
            lambda n: (2 * core + n // 64) * 4 + n % 4,
            lambda n: (n % 64) // 4,
            lambda r, n: (r == 6) | (r == 7),
        )
        both_rows = fold(lambda a, r: a == r - 6, wide)
        qv_vec[2 * chunk] = both_rows[0:1]
        qv_vec[2 * chunk + 1] = both_rows[1:2]
        wide = spread(
            512,
            lambda n: 8 * core + n // 64,
            lambda n: (n % 64) // 4,
            lambda r, n: r == 8 + n % 4,
        )
        one_row = fold(lambda a, r: (a == 0) & (r >= 0), wide)
        up_vec[2 * chunk] = one_row[0:1, :256]
        up_vec[2 * chunk + 1] = one_row[0:1, 256:]

    def vector(r):
        return norm_vec[r : r + 1, :]

    def span(i, size, align=None):
        if isinstance(i, int):
            return pl.ds(i * size, size)
        return pl.ds(pl.multiple_of(i * size, align or size), size)

    def tile(t):
        return span(t, TILE, 16)

    def both(number, rows):
        return own[rows, :].astype(F32) + part[number % 2, rows, :].astype(F32)

    def normed(value):
        centred = value - jnp.mean(value, axis=-1, keepdims=True)
        spread = jnp.mean(centred * centred, axis=-1, keepdims=True)
        scale = lax.rsqrt(spread + EPSILON)
        return centred * scale, scale

    def by_n(group, n, cut=slice(None)):
        return jnp.concatenate([w[group, g, n].reshape(256, 512)[:, cut] for g in range(4)], axis=1)

    def add_sum(row, value):
        s.sums[row] += value.reshape(value.shape[0] // 8, 8, D).sum(0)

    head_of = iota((1, 128), 1) // 64
    head_mask = [(head_of == j).astype(F32).astype(BF) for j in range(2)]

    def pick(a, b):
        return jnp.where(iota(a.shape, 1) < 64, a, b)

    def section_copy(slot, t, src):
        rows = tile(t)
        return send(src.at[rows], rows_in.at[slot, rows], (s.sec_s.at[t], s.sec_r.at[t]), other_section)

    def section_cross(slot, t):
        ref = rows_in.at[slot, tile(t)]
        return send(ref, ref, (s.sec_cross_s.at[t], s.sec_cross_r.at[t]), other_core)

    def section_pair(slot, k, use):
        mine, theirs = 2 * k + core, 2 * k + 1 - core
        section_copy(slot, mine, own).wait_recv()
        section_cross(slot, mine).start()
        use(mine)
        section_cross(slot, theirs).wait_recv()
        use(theirs)

    def section_forwarded(slot):
        for k in range(N_TILES // 2):
            section_cross(slot, 2 * k + core).wait_send()

    def section_send(slot, t, src):
        @pl.when(core == lax.rem(t, 2) if not isinstance(t, int) else core == t % 2)
        def _():
            section_copy(slot, t, src).start()

    def section_sent(slot, src):
        for k in range(N_TILES // 2):
            section_copy(slot, 2 * k + core, src).wait_send()

    def result_copy(src, owner):
        micro, owner_core = z // 2, lax.rem(z, 2)
        cols = pl.ds(pl.multiple_of(core * 512, 512), 512)
        from_ref = src.at[pl.ds(owner * TILE, TILE), cols]
        stays = jnp.logical_and(owner == z, core == owner_core)
        where = {CORE: owner_core, TENSOR: jnp.int32(owner)}
        to_ref = out_rows.at[micro, :, cols]
        sems = (s.res_s.at[owner], s.res_r.at[micro, core])
        return stays, send(from_ref, to_ref, sems, where), pltpu.make_async_copy(from_ref, to_ref, sems[1])

    def result_send(src):
        for owner in range(4):
            stays, away, stay = result_copy(src, owner)

            @pl.when(stays)
            def _():
                stay.start()

            @pl.when(jnp.logical_not(stays))
            def _():
                away.start()

    def result_sent(src):
        for owner in range(4):
            stays, away, stay = result_copy(src, owner)

            @pl.when(jnp.logical_not(stays))
            def _():
                away.wait_send()

    def norm_one(t):
        rows = tile(t)
        value, _ = normed(rows_in[0, rows, :].astype(F32))
        h1[rows, :] = (value * vector(0) + vector(1)).astype(BF)

    def project(pair, r):
        rows = span(r, HALF, 16)
        a, b = 2 * pair, 2 * pair + 1
        wa, wb = w[0, a].reshape(D, 512), w[0, b].reshape(D, 512)
        for half, weights in ((a, wa[:, :256]), (b, wb[:, :256])):
            p = dot(h1[rows, :], weights)
            qkv[half, 0, rows] = ((p[:, :128] + qv_vec[2 * half]) * 0.125).astype(BF)
            qkv[half, 1, rows] = p[:, 128:].astype(BF)
        p = dot(h1[rows, :], jnp.concatenate([wa[:, 256:384], wb[:, 256:384]], axis=1))
        qkv[a, 2, rows] = (p[:, :128] + qv_vec[2 * a + 1]).astype(BF)
        qkv[b, 2, rows] = (p[:, 128:] + qv_vec[2 * b + 1]).astype(BF)

    def attend(g):
        query, key, value = qkv[g, 0], qkv[g, 1], qkv[g, 2]
        outs = []
        for j in range(2):
            scores = dot_nt(key * head_mask[j], query)
            e = jnp.exp(scores - jnp.max(scores, axis=0, keepdims=True))
            p = (e * (1.0 / jnp.sum(e, axis=0, keepdims=True))).astype(BF)
            probs[2 * g + j] = p
            outs.append(dot_tn(p, value))
        o[:, span(g, 128)] = pick(*outs).astype(BF)

    def out_part(n):
        own[:, span(n, 256)] = dot_nt(o[...], by_n(0, n, slice(384, 512))).astype(BF)

    def norm_two(t):
        rows = tile(t)
        middle = rows_in[0, rows, :].astype(F32) + both(0, rows) + vector(2)
        r1[rows, :] = middle
        value, _ = normed(middle)
        h2[rows, :] = (value * vector(3) + vector(4)).astype(BF)

    def feed(i, with_grad=False):
        g, half = (i // 2, i % 2) if isinstance(i, int) else (i // 2, lax.rem(i, 2))
        weights = w[1, g, :, :, :, span(half, 256)].reshape(D, 256)
        for t in range(2):
            rows = pl.ds(t * 288, 288)
            u = dot(h2[rows, :], weights) + up_vec[i]
            phi = 0.5 + 0.5 * lax.erf(u * (2.0**-0.5))
            act[rows, span(i, 256)] = (u * phi).astype(BF)
            slope = phi + u * jnp.exp(u * u * -0.5) * 0.3989422804014327
            if with_grad:
                slope = slope * pull[rows, span(i, 256)].astype(F32)
            slope = slope.astype(BF)
            pull[rows, span(i, 256)] = slope
            if with_grad:
                add_bias(i, t, slope)

    def down(r, n):
        rows = span(r, HALF, 16)
        own[rows, span(n, 256)] = dot_nt(act[rows, :], by_n(2, n)).astype(BF)

    def finish(t):
        rows = tile(t)
        out_b[rows, :] = (r1[rows, :] + both(1, rows) + vector(5)).astype(BF)

    def add_bias(i, r, value):
        value = jnp.sum(value.astype(F32), axis=0, keepdims=True)
        s.up_grad[i] = value if r == 0 else s.up_grad[i] + value

    def feed_grad(i, rows):
        g, half = (i // 2, i % 2) if isinstance(i, int) else (i // 2, lax.rem(i, 2))
        return dot(rows_in[1, rows, :], w[2, g, :, :, :, span(half, 256)].reshape(D, 256))

    def feed_early(i):
        pull[:, span(i, 256)] = feed_grad(i, slice(None)).astype(BF)

    def feed_back(r, i):
        rows = pl.ds(r * HALF, HALF)
        du = (feed_grad(i, rows) * pull[rows, span(i, 256)].astype(F32)).astype(BF)
        pull[rows, span(i, 256)] = du
        add_bias(i, r, du)

    def up_back(n):
        own[:, span(n, 256)] = dot_nt(pull[...], by_n(1, n)).astype(BF)

    def norm_back(value, grad, gain, gain_row, shift_row):
        hat, scale = normed(value)
        add_sum(gain_row, grad * hat)
        add_sum(shift_row, grad)
        dy = grad * gain
        return scale * (
            dy - jnp.mean(dy, axis=-1, keepdims=True) - hat * jnp.mean(dy * hat, axis=-1, keepdims=True)
        )

    def norm_two_back(t):
        rows = tile(t)
        pulled = norm_back(r1[rows, :], both(2, rows), vector(3), 3, 4)
        gy = rows_in[1, rows, :].astype(F32)
        grad = gy + pulled
        add_sum(5, gy)
        add_sum(2, grad)
        r1[rows, :] = grad
        gr[rows, :] = grad.astype(BF)

    def out_back(pair):
        weights = [w[0, 2 * pair + j, :, :, :, 384:512].reshape(D, 128) for j in range(2)]
        do[:, span(pair, 256)] = dot(gr[...], jnp.concatenate(weights, axis=1)).astype(BF)

    def attend_back(g):
        query, key, value = qkv[g, 0], qkv[g, 1], qkv[g, 2]
        grad = do[:, span(g, 128)]
        dq, dk, dv = [], [], []
        for j in range(2):
            p = probs[2 * g + j]
            dv.append(dot(p, grad))
            dp = dot_nt(value * head_mask[j], grad)
            p = p.astype(F32)
            ds = (p * (dp - jnp.sum(dp * p, axis=0, keepdims=True))).astype(BF)
            dk.append(dot(ds, query))
            dq.append(dot_tn(ds, key))
        dq, dk, dv = (pick(*pair).astype(BF) for pair in (dq, dk, dv))
        dq = dq * jnp.asarray(0.125, BF)
        qkv[g, 0] = dq
        qkv[g, 1] = dk
        qkv[g, 2] = dv
        s.qv_grad[2 * g] = jnp.sum(dq.astype(F32), axis=0, keepdims=True)
        s.qv_grad[2 * g + 1] = jnp.sum(dv.astype(F32), axis=0, keepdims=True)

    def qkv_all(first_g, last_g, rows=slice(None)):
        return jnp.concatenate([qkv[g, k, rows] for g in range(first_g, last_g) for k in range(3)], axis=1)

    def project_back(r, n):
        rows = span(r, HALF, 16)
        own[rows, span(n, 256)] = dot_nt(qkv_all(0, 4, rows), by_n(0, n, slice(0, 384))).astype(BF)

    def norm_one_back(t):
        rows = tile(t)
        pulled = norm_back(rows_in[0, rows, :].astype(F32), both(3, rows), vector(0), 0, 1)
        own[rows, :] = (r1[rows, :] + pulled).astype(BF)

    def zero_sums():
        s.sums[...] = jnp.zeros_like(s.sums)

    def fill_vec():
        vec[...] = jnp.zeros_like(vec)
        for r in range(6):
            vec[r : r + 1, :] = jnp.sum(s.sums[r], axis=0, keepdims=True)
        for r in range(8):
            vec[8 + r : 9 + r, 512:640] = s.qv_grad[r]
            vec[8 + r // 2 : 9 + r // 2, r % 2 * 256 : r % 2 * 256 + 256] = s.up_grad[r]

    def grads(group, m):
        def left(ref):
            return ref[:, m * 256 : m * 256 + 256].T

        def put(g, col, value):
            cols = value.shape[1]
            w[group, g, m, :, :, col : col + cols] = value.astype(BF).reshape(2, 128, cols)

        if group == 0:
            first_left = left(h1)
            for pair in range(2):
                out = dot(first_left, qkv_all(2 * pair, 2 * pair + 2))
                put(2 * pair, 0, out[:, :384])
                put(2 * pair + 1, 0, out[:, 384:])
        else:
            rows, right = (h2, pull) if group == 1 else (rows_in.at[1], act)
            rows_t = left(rows)
            for g in range(4):
                put(g, 0, dot(rows_t, right[:, g * 512 : g * 512 + 512]))

    def out_grads(m):
        out = dot(gr[:, m * 256 : m * 256 + 256].T, o[...]).astype(BF)
        for g in range(4):
            w[0, g, m, :, :, 384:512] = out[:, g * 128 : g * 128 + 128].reshape(2, 128, 128)

    def part_steps(number, body, cost, waits):
        return [
            Step(waits if n == 0 else [], cost, [((PART, number, n), CORE, 295000)], partial(body, n))
            for n in range(4)
        ]

    def half_steps(number, body, cost, waits):
        return [
            Step(
                waits if (r, n) == (0, 0) else [],
                cost,
                [((PART, number, r), CORE, 590000)] if n == 3 else (),
                partial(body, r, n),
            )
            for r in range(2)
            for n in range(4)
        ]

    def norm_steps(number, body, cost, after=None):
        def one(t, pieces):
            for n in pieces:
                part_copy(number, n).wait_send()
            body(t)
            if after is not None:
                after(t)

        steps = []
        for t in range(N_TILES):
            if number % 2:
                pieces = [t // 2] if t % 2 == 0 else []
            else:
                pieces = list(range(4)) if t == 0 else []
            steps.append(Step([(PART, number, n) for n in pieces], cost, (), partial(one, t, pieces)))
        return steps

    def everything(group):
        return [(group, order) for order in range(4)]

    forward = []
    forward += [Step([(READY, 1)] if t == 0 else [], 0.5, (), partial(norm_one, t)) for t in range(N_TILES)]
    forward += [Step(everything(0), 0.7, (), partial(project, p, r)) for p in range(2) for r in range(2)]
    forward += [Step([], 1.6, (), partial(attend, g)) for g in range(4)]
    forward += part_steps(0, out_part, 0.4, [])
    forward += norm_steps(0, norm_two, 0.6)
    forward += [Step(everything(1), 0.6, (), partial(feed, i)) for i in range(8)]
    forward += half_steps(1, down, 0.5, everything(2))
    forward += norm_steps(1, finish, 0.3, lambda t: section_send(0, t, out_b))
    forward = [step._replace(where=first) for step in forward]
    unpacking = [Step([(SMALL, 0)], 1.5, (), partial(unpack, chunk)) for chunk in range(4)]
    edge_steps = [
        Step([], 0.2, EDGE_TASKS, edge_start),
        Step([(0, 3)], 0.2, [CROSS_TASK], edge_arrived),
        Step([CROSS_TASK[0]], 0.2, [note(READY, 1)], edge_done),
    ]
    gathers = [gather_chain(SMALL, 0)] + [gather_chain(g, o) for g in range(3) for o in range(4)]
    emit(gathers + [edge_steps, unpacking + forward])
    sent_all()

    def loop(count, body):
        def one(i, carry):
            body(i)
            return carry

        lax.fori_loop(0, count, one, 0)

    def exchange(number, body):
        def one(n):
            body(n)
            part_copy(number, n).start()

        loop(4, one)
        loop(4, lambda n: part_copy(number, n).wait())

    zero_sums()

    def exchange_halves(number, body, use):
        for r in range(2):
            loop(4, partial(body, r))
            part_copy(number, r).start()
        for r in range(2):
            part_copy(number, r).wait()
            loop(2, lambda t: use(2 * r + t))

    @pl.when(sec == 1)
    def _():
        loop(8, feed_early)
        for k in range(N_TILES // 2):
            section_pair(0, k, norm_one)
            loop(2, lambda pair: project(pair, k))
        loop(4, attend)
        exchange(0, out_part)
        loop(4, norm_two)
        loop(8, partial(feed, with_grad=True))
        exchange_halves(1, down, finish)
        result_send(out_b)
        exchange(2, up_back)
        loop(4, norm_two_back)
        loop(2, out_back)
        loop(4, attend_back)

        def last(t):
            norm_one_back(t)
            section_send(1, t, own)

        exchange_halves(3, project_back, last)
        section_forwarded(0)

    def reduce_add(group, order, op):
        axis, kind = op
        if kind == "end":
            kinds = ("s",) if axis == X else ("s+", "s-")
            at_axis, half = here[axis], None
        else:
            kinds = (kind,)
            at_axis = beside(axis, 1 if kind == "h+" else -1)
            half = 0 if kind == "h+" else 1
        at, later, row, rows, col, cols = reduce_place(group, order, axis, at_axis, half)
        open_axes = [a for a in (Z, Y, X) if a in later]
        count = 1
        for a in open_axes:
            count *= SIZE[a]

        def one(i):
            rest, index = i, dict(at)
            for a in reversed(open_axes):
                index[a] = lax.rem(rest, SIZE[a])
                rest = rest // SIZE[a]
            lead = tuple(index[a] for a in open_axes)
            place = (group, index[Z], index[Y], index[X], pl.ds(row, rows), pl.ds(col, cols))
            value = w[place].astype(F32)
            for k in kinds:
                value += landing[(order, axis, k)][(group, *lead, pl.ds(0, rows), slice(None))].astype(F32)
            if later or kind != "end":
                w[place] = value.astype(BF)
            else:
                total[group, pl.ds(row, rows), :] = value

        if count == 1:
            one(0)
        else:
            loop(count, one)

    def vec_add(axis):
        value = vec[...]
        for step in range(1, SIZE[axis]):
            vec_copy(axis, step).wait_send()
            value += vec_in[VEC_SLOT[axis] + step - 1]
        vec[...] = value
        if axis == X:
            out_vectors[0] = value

    def vec_last():
        vec_copy(CORE, 1).wait_send()
        out_vectors[1] = vec_in[7]

    def vec_tasks(axis):
        return [((VEC, axis, step), VEC, 100000) for step in range(1, SIZE[axis])]

    def vec_waits(axis):
        return [(VEC, axis, step) for step in range(1, SIZE[axis])]

    vec_chain = [
        Step([(READY, 4)], 0.3, vec_tasks(Y), fill_vec),
        Step(vec_waits(Y), 0.2, vec_tasks(Z), lambda: vec_add(Y)),
        Step(vec_waits(Z), 0.2, vec_tasks(X), lambda: vec_add(Z)),
        Step(vec_waits(X), 0.2, [((VEC, CORE, 1), CORE, 65536)], lambda: vec_add(X)),
        Step([(VEC, CORE, 1)], 0.1, (), vec_last),
    ]

    def final_copy(group):
        src = total.at[group, pl.ds(pl.multiple_of((1 - core) * 64, 64), 64), :]
        return send(src, out_weights.at[group, core], (s.fin_s.at[group], s.fin_r.at[group]), other_core)

    def final_local(group):
        src = total.at[group, pl.ds(pl.multiple_of(core * 64, 64), 64), :]
        return pltpu.make_async_copy(src, out_weights.at[group, core], s.local.at[group])

    def final_start(group):
        final_copy(group).start()
        final_local(group).start()

    finals = [
        [Step([(TOTAL, group, order) for order in range(4)], 0.1, (), partial(final_start, group))]
        for group in (2, 1, 0)
    ]

    def only_first(steps):
        return [step._replace(where=first) for step in steps]

    def grad_steps(group, cost):
        return [
            Step([], cost, [note(GRADS, group)] if m == 3 else (), partial(grads, group, m)) for m in range(4)
        ]

    backward = []
    for k in range(N_TILES // 2):
        backward += only_first([Step([], 0.0, (), partial(section_pair, 1, k, lambda t: None))])
        backward += only_first([Step([], 0.25, (), partial(feed_back, k, i)) for i in range(8)])
    backward += only_first([Step([], 0.0, (), partial(section_forwarded, 1))])
    backward += grad_steps(2, 0.9)
    backward += only_first(part_steps(2, up_back, 0.8, []))
    backward += grad_steps(1, 1.0)
    backward += only_first(norm_steps(2, norm_two_back, 0.8))
    backward += only_first([Step([], 0.5, (), partial(out_back, p)) for p in range(2)])
    backward += only_first([Step([], 2.0, (), partial(attend_back, g)) for g in range(4)])
    backward += only_first(half_steps(3, project_back, 0.35, []))
    backward += [Step([], 0.5, (), partial(out_grads, m)) for m in range(4)]
    backward += grad_steps(0, 1.0)
    backward += only_first(norm_steps(3, norm_one_back, 0.8))
    backward += only_first([Step([], 0.1, (), lambda: result_send(own))])
    backward += [Step([], 0.0, [note(READY, 4)])]
    reduces = [reduce_chain(g, o, reduce_add) for g in (2, 1, 0) for o in range(4)]
    emit(reduces + finals + [vec_chain, backward], latency=3.0)
    sent_all()

    for group in range(3):
        final_local(group).wait()
        final_copy(group).wait()

    @pl.when(first)
    def _():
        section_sent(0, out_b)
        result_sent(own)

    @pl.when(sec == 1)
    def _():
        section_sent(1, own)
        result_sent(out_b)

    for micro in range(2):
        for half in range(2):
            dst = out_rows.at[micro, :, pl.ds(half * 512, 512)]
            pltpu.make_async_copy(dst, dst, s.res_r.at[micro, half]).wait()


def dma(*shape):
    return pltpu.SemaphoreType.DMA(shape)


SCRATCH = dict(
    blocks=pltpu.VMEM((2, 3, 64, 512), BF),
    w=pltpu.VMEM((3, 4, 4, 2, 128, 512), BF),
    rows_in=pltpu.VMEM((2, T, D), BF),
    h1=pltpu.VMEM((T, D), BF),
    h2=pltpu.VMEM((T, D), BF),
    qkv=pltpu.VMEM((4, 3, T, 128), BF),
    o=pltpu.VMEM((T, 512), BF),
    r1=pltpu.VMEM((T, D), F32),
    act=pltpu.VMEM((T, 2048), BF),
    pull=pltpu.VMEM((T, 2048), BF),
    probs=pltpu.VMEM((8, T, T), BF),
    part=pltpu.VMEM((2, T, D), BF),
    own=pltpu.VMEM((T, D), BF),
    out_b=pltpu.VMEM((T, D), BF),
    gr=pltpu.VMEM((T, D), BF),
    do=pltpu.VMEM((T, 512), BF),
    tiles=pltpu.VMEM((4, 4, 2, 2, 16, 128), BF),
    norm_vec=pltpu.VMEM((8, D), F32),
    qv_vec=pltpu.VMEM((8, 1, 128), F32),
    up_vec=pltpu.VMEM((8, 1, 256), F32),
    sums=pltpu.VMEM((6, 8, D), F32),
    qv_grad=pltpu.VMEM((8, 1, 128), F32),
    up_grad=pltpu.VMEM((8, 1, 256), F32),
    vec=pltpu.VMEM((16, D), F32),
    vec_in=pltpu.VMEM((8, 16, D), F32),
    total=pltpu.VMEM((3, 128, 512), F32),
    local=dma(4),
    swap_s=dma(4),
    swap_r=dma(4),
    edge_s=dma(2, 2),
    edge_r=dma(4),
    cross=dma(2),
    small_s=dma(N_SMALL),
    small_r=dma(N_SMALL),
    link_s=dma(3, N_TASKS),
    gather_r=dma(3, N_TASKS),
    reduce_r=dma(3, N_TASKS),
    part_s=dma(4, N_TILES),
    part_r=dma(4, N_TILES),
    sec_s=dma(N_TILES),
    sec_r=dma(N_TILES),
    sec_cross_s=dma(N_TILES),
    sec_cross_r=dma(N_TILES),
    res_s=dma(4),
    res_r=dma(2, 2),
    vec_s=dma(8),
    vec_r=dma(8),
    fin_s=dma(3),
    fin_r=dma(3),
)


def finish_kernel(rows, weights, vectors, ends, qkv, qv, out, up, up_bias, down, norm):
    core, z = lax.axis_index(CORE), lax.axis_index(TENSOR)
    position = (lax.axis_index(DP_Y) * 2 + lax.axis_index(DP_X)) * 2 + core
    ends[...] = rows[...].astype(F32)
    for half in range(2):
        narrow, wide = slice(half * 128, half * 128 + 128), slice(half * 512, half * 512 + 512)
        for k in range(3):
            qkv[k, :, narrow] = weights[0, half, :, k * 128 : k * 128 + 128]
        out[:, narrow] = weights[0, half, :, 384:512]
        up[:, wide] = weights[1, half]
        down[:, wide] = weights[2, half]
    mine = pltpu.roll(vectors[0], D - (position * 4 + z) * 16, 1)
    for r in range(6):
        norm[r] = mine[r : r + 1, :16]
    bias = jnp.zeros((8, 128), F32)
    for half in range(2):
        own = jnp.where(core == half, vectors[0], vectors[1])
        heads = pltpu.roll(pltpu.roll(own[8:16, 512:640], 128 - position * 4, 1), 8 - 2 * z, 0)
        hidden = pltpu.roll(pltpu.roll(own[8:16, :512], 512 - position * 4, 1), 8 - z, 0)
        for j in range(2):
            for part in range(2):
                qv[part, 2 * half + j : 2 * half + j + 1, :] = heads[part : part + 1, 64 * j : 64 * j + 4]
        row, lane = (lax.broadcasted_iota(jnp.int32, (8, 512), i) for i in range(2))
        spread = jnp.where(lane % 64 == row, jnp.broadcast_to(hidden[0:1], (8, 512)), 0.0)
        lane, column = (lax.broadcasted_iota(jnp.int32, (512, 128), i) for i in range(2))
        gather = (lane // 64 + 8 * half == column).astype(F32)
        bias += jnp.dot(spread, gather, precision=lax.Precision.HIGHEST, preferred_element_type=F32)
    up_bias[...] = bias[:4, :16]


def body(boundary, w_qkv, qv_bias, w_out, up_weight, up_bias, down_weight, norm_bias):
    anywhere = pl.BlockSpec(memory_space=pl.ANY)
    vmem = pl.BlockSpec(memory_space=pltpu.VMEM)
    small = jnp.concatenate([norm_bias[0], qv_bias[0].reshape(2, 16), up_bias[0].T])
    small = jnp.pad(small, ((0, 4), (0, 112)))
    results = pl.pallas_call(
        kernel,
        out_shape=(
            jax.ShapeDtypeStruct((2, TILE, D), BF),
            jax.ShapeDtypeStruct((3, 2, 64, 512), F32),
            jax.ShapeDtypeStruct((2, 16, D), F32),
        ),
        in_specs=[anywhere] + [vmem] * 5,
        out_specs=(anywhere, anywhere, vmem),
        scratch_shapes=[*SCRATCH.values(), *(pltpu.VMEM(shape, BF) for shape in LANDINGS.values())],
        compiler_params=pltpu.CompilerParams(
            collective_id=0, has_side_effects=True, vmem_limit_bytes=62 << 20
        ),
    )(boundary[0, :, 0], small, jnp.moveaxis(w_qkv[0], 1, 0), w_out[0].T, up_weight[0], down_weight[0].T)
    shapes = ((2, TILE, D), (3, 64, 256), (2, 4, 4), (64, 256), (64, 1024), (4, 16), (64, 1024), (6, 1, 16))
    ends, qkv, qv, out, up, up_bias_grad, down, norm = pl.pallas_call(
        finish_kernel,
        out_shape=tuple(jax.ShapeDtypeStruct(shape, F32) for shape in shapes),
        in_specs=[vmem] * 3,
        out_specs=(vmem,) * 8,
    )(*results)
    results = (jnp.moveaxis(qkv, 0, 1), qv, out.T, up, up_bias_grad.T, down.T, norm[:, 0])
    return (ends[None, :, None], *(result[None] for result in results))


def solution(mesh):
    torus = Mesh(mesh.devices.reshape(mesh.shape[SECTION], 4, 2, 2, mesh.shape[TENSOR]), AXES)
    in_specs = (
        P(SECTION, None, DP, TENSOR, None),
        P(SECTION, DP, None, TENSOR),
        P(SECTION, None, TENSOR, DP),
        P(SECTION, TENSOR, DP),
        P(SECTION, DP, TENSOR),
        P(SECTION, TENSOR, DP),
        P(SECTION, TENSOR, DP),
        P(SECTION, None, DP_TENSOR),
    )
    return jax.shard_map(body, mesh=torus, in_specs=in_specs, out_specs=in_specs, check_vma=False)
```

```python
from functools import partial
from types import SimpleNamespace
from typing import Any, NamedTuple

import jax
import jax.numpy as jnp
from jax import lax
from jax.experimental import pallas as pl
from jax.experimental.pallas import tpu as pltpu
from jax.sharding import Mesh
from jax.sharding import PartitionSpec as P

AXES = SECTION, DP_Y, DP_X, CORE, TENSOR = ("section", "dp_0", "dp_1", "dp_2", "tensor")
DP = (DP_Y, DP_X, CORE)
DP_TENSOR = (DP_Y, DP_X, CORE, TENSOR)
MESH = pl.DeviceIdType.MESH
BF, F32 = jnp.bfloat16, jnp.float32

X, Y, Z = "x", "y", "z"
SMALL, GRADS, TOTAL, PART, VEC, READY = "small", "grads", "total", "part", "vec", "ready"
EPSILON = 1e-06
T = 576
D = 1024
TILE = 144
HALF = 288
N_TILES = T // TILE
SIZE = {Y: 4, X: 2, Z: 4}
NAME = {Y: DP_Y, X: DP_X, Z: TENSOR}

ORDERS = ((X, Y, Z), (X, Z, Y), (Y, Z, X), (Z, Y, X))
ROWS = ((48, 48, 16, 16), (48, 32, 32, 16), (32, 48, 16, 32))
MAX_ROWS = (48, 48, 32, 32)

NT = (((1,), (1,)), ((), ()))
TN = (((0,), (0,)), ((), ()))


def dot(a, b):
    return jnp.dot(a, b, preferred_element_type=F32)


def dot_nt(a, b):
    return lax.dot_general(a, b, NT, preferred_element_type=F32)


def dot_tn(a, b):
    return lax.dot_general(a, b, TN, preferred_element_type=F32)


class Step(NamedTuple):
    waits: list
    cost: float = 0.0
    sends: list = ()
    op: Any = None
    where: Any = None


RATE, LATENCY = 49000.0, 1.5


def in_order(chains, rate=RATE, latency=LATENCY):
    link_free = {}
    arrives = {}
    clock = 0.0
    place = [0] * len(chains)
    order = []
    while True:
        best = None
        for index, chain in enumerate(chains):
            if place[index] == len(chain):
                continue
            step = chain[place[index]]
            if any(task not in arrives for task in step.waits):
                continue
            ready = max([arrives[task] for task in step.waits], default=0.0)
            ready = max(ready, clock)
            if best is None or ready < best[0] - 1e-9:
                best = (ready, index)
        if best is None:
            assert all(p == len(c) for p, c in zip(place, chains))
            return order
        ready, index = best
        step = chains[index][place[index]]
        place[index] += 1
        clock = ready + step.cost
        for task, link, size in step.sends:
            if link is None:
                arrives[task] = clock
                continue
            begin = max(clock, link_free.get(link, 0.0))
            fast = 6.0 if link == CORE else 1.0
            link_free[link] = begin + size / rate / fast
            arrives[task] = link_free[link] + latency
            clock += 0.05
        order.append(step)


def note(*key):
    return (key, None, 0)


EDGE_TASKS = [((READY, 2), READY, 295000)]
CROSS_TASK = ((READY, 3), CORE, 590000)


def bytes_of(done, axis_fixed, rows, columns):
    blocks = 1
    for axis in done:
        blocks *= SIZE[axis]
    return blocks * rows * columns * 2


def gather_chain(group, order):
    rows = 8 if group == SMALL else ROWS[group][order]
    steps, waits, done = [], [], []
    for axis in ORDERS[order]:
        full = bytes_of(done, axis, rows, 512)
        key = (group, order, axis)
        if axis == X:
            steps.append(Step(waits, 0.0, [(key + ("s",), X, full)]))
            waits = [key + ("s",)]
        else:
            steps.append(Step(waits, 0.0, [(key + ("s+",), axis + "+", full), (key + ("s-",), axis + "-", full)]))
            steps.append(Step([key + ("s+",)], 0.0, [(key + ("f+",), axis + "+", full / 2)]))
            steps.append(Step([key + ("s-",)], 0.0, [(key + ("f-",), axis + "-", full / 2)]))
            waits = [key + ("f+",), key + ("f-",)]
        done.append(axis)
    if group != SMALL:
        last = next(i for i, step in enumerate(steps) if step.sends[0][0][2] == axis)
        if group:
            steps[last] = steps[last]._replace(waits=[*steps[last].waits, (READY, 0, order)])
        steps[-1].sends.append(note(READY, group, order))
    steps.append(Step(waits, 0.0, [note(group, order)]))
    return steps


def reduce_chain(group, order, add):
    rows = ROWS[group][order]
    steps, end, cost = [], None, 0.0
    waits = [(GRADS, group)]
    left = list(ORDERS[order])
    per = 0.3e-6

    def step(waits, cost, op, sends):
        run = None if op is None else (lambda: add(group, order, op))
        steps.append(Step(waits, cost, sends, run))

    while left:
        axis = left.pop()
        full = bytes_of(left, axis, rows, 512)
        key = (GRADS, group, order, axis)
        if axis == X:
            step(waits, cost, end, [(key + ("s",), X, full)])
            waits = [key + ("s",)]
        else:
            step(waits, cost, end, [(key + ("h+",), axis + "+", full / 2), (key + ("h-",), axis + "-", full / 2)])
            step([key + ("h+",)], 0.1 + full / 4 * per, (axis, "h+"), [(key + ("s+",), axis + "+", full)])
            step([key + ("h-",)], 0.1 + full / 4 * per, (axis, "h-"), [(key + ("s-",), axis + "-", full)])
            waits = [key + ("s+",), key + ("s-",)]
        end = (axis, "end")
        cost = 0.1 + full * per
    step(waits, cost, end, [note(TOTAL, group, order)])
    return steps


GATHER_TASKS = {}
REDUCE_TASKS = {}
for _axes in ORDERS:
    for _axis in _axes:
        for _kind in ("s",) if _axis == X else ("s+", "s-", "f+", "f-"):
            GATHER_TASKS.setdefault((_axes, _axis, _kind), len(GATHER_TASKS))
        for _kind in ("s",) if _axis == X else ("s+", "s-", "h+", "h-"):
            REDUCE_TASKS.setdefault((_axes, _axis, _kind), len(REDUCE_TASKS))
N_TASKS = len(GATHER_TASKS)
N_SMALL = 9


def landing_shapes():
    shapes = {}
    for order, axes in enumerate(ORDERS):
        left = list(axes)
        while left:
            axis = left.pop()
            lead = tuple(SIZE[a] for a in (Z, Y, X) if a in left)
            for kind in ("s",) if axis == X else ("s+", "s-", "h+", "h-"):
                columns = 256 if kind[0] == "h" else 512
                shapes[(order, axis, kind)] = (3, *lead, MAX_ROWS[order], columns)
    return shapes


LANDINGS = landing_shapes()


def kernel(edge, small, qkv_in, out_in, up_in, down_in, out_rows, out_weights, out_vectors, *scratch):
    s = SimpleNamespace(**dict(zip(SCRATCH, scratch)))
    landing = dict(zip(LANDINGS, scratch[len(SCRATCH) :]))
    w, rows_in, h1, h2, qkv, o = s.w, s.rows_in, s.h1, s.h2, s.qkv, s.o
    r1, act, pull, probs = s.r1, s.act, s.pull, s.probs
    part, own, out_b, gr, do = s.part, s.own, s.out_b, s.gr, s.do
    tiles, norm_vec, qv_vec, up_vec = s.tiles, s.norm_vec, s.qv_vec, s.up_vec
    vec, vec_in, total = s.vec, s.vec_in, s.total

    sec = lax.axis_index(SECTION)
    y, x, core, z = (lax.axis_index(n) for n in (DP_Y, DP_X, CORE, TENSOR))
    here = {Y: y, X: x, Z: z}
    first = sec == 0

    def beside(axis, step):
        return lax.rem(here[axis] + step + SIZE[axis], SIZE[axis])

    def device(axis, step):
        return {NAME[axis]: beside(axis, step)}

    other_core = {CORE: 1 - core}
    other_section = {SECTION: 1 - sec}

    def send(src, dst, sems, where):
        return pltpu.make_async_remote_copy(
            src_ref=src, dst_ref=dst, send_sem=sems[0], recv_sem=sems[1], device_id=where, device_id_type=MESH
        )

    barrier = pltpu.get_barrier_semaphore()
    peers = [device(Y, 1), device(Y, 2), device(Y, 3), device(X, 1), other_section]
    peers += [device(Z, step) for step in (1, 2, 3)] + [other_core]
    peers += [{CORE: 1 - core, TENSOR: beside(Z, step)} for step in (1, 2, 3)]
    for peer in peers:
        pl.semaphore_signal(barrier, inc=1, device_id=peer, device_id_type=MESH)
    blocks_in = s.blocks
    for half in range(2):
        narrow, wide = pl.ds(half * 128, 128), pl.ds(half * 512, 512)
        for k in range(3):
            blocks_in[half, 0, :, k * 128 : k * 128 + 128] = qkv_in[k, :, narrow]
        blocks_in[half, 0, :, 384:512] = out_in[:, narrow]
        blocks_in[half, 1] = up_in[:, wide]
        blocks_in[half, 2] = down_in[:, wide]
    pl.semaphore_wait(barrier, len(peers))

    def own_rows(group):
        return w.at[group, z, y, x, pl.ds(pl.multiple_of(core * 64, 64), 64), :]

    local = [pltpu.make_async_copy(blocks_in.at[core, g], own_rows(g), s.local.at[g]) for g in range(3)]
    local.append(pltpu.make_async_copy(small, tiles.at[z, y, x, core], s.local.at[3]))
    swap = [
        send(blocks_in.at[1 - core, g], own_rows(g), (s.swap_s.at[g], s.swap_r.at[g]), other_core)
        for g in range(3)
    ]
    swap.append(send(small, tiles.at[z, y, x, core], (s.swap_s.at[3], s.swap_r.at[3]), other_core))
    for copy in swap + local:
        copy.start()

    def edge_copy(micro, half):
        to = 2 * micro + core
        src = edge.at[micro, :, pl.ds(half * 512, 512)]
        dst = rows_in.at[sec, pl.ds(pl.multiple_of(z * TILE, TILE), TILE), pl.ds(half * 512, 512)]
        stays = jnp.logical_and(to == z, core == half)
        where = {CORE: half, TENSOR: to}
        away = send(src, dst, (s.edge_s.at[micro, half], s.edge_r.at[z]), where)
        stay = pltpu.make_async_copy(src, dst, s.edge_r.at[z])
        return stays, away, stay

    def edge_start():
        for micro in range(2):
            for half in range(2):
                stays, away, stay = edge_copy(micro, half)

                @pl.when(stays)
                def _():
                    stay.start()

                @pl.when(jnp.logical_not(stays))
                def _():
                    away.start()

    half_image = rows_in.at[sec, :, pl.ds(pl.multiple_of(core * 512, 512), 512)]

    def cross():
        return send(half_image, half_image, (s.cross.at[0], s.cross.at[1]), other_core)

    def edge_arrived():
        for source in range(4):
            dst = rows_in.at[sec, pl.ds(source * TILE, TILE), pl.ds(pl.multiple_of(core * 512, 512), 512)]
            pltpu.make_async_copy(dst, dst, s.edge_r.at[source]).wait()
        cross().start()

    def edge_done():
        cross().wait()
        for micro in range(2):
            for half in range(2):
                stays, away, _ = edge_copy(micro, half)

                @pl.when(jnp.logical_not(stays))
                def _():
                    away.wait_send()

    for copy in local:
        copy.wait()
    for copy in swap:
        copy.wait()

    def region(group, at, row, rows, col, cols):
        index = [at[a] if at.get(a) is not None else slice(None) for a in (Z, Y, X)]
        return w.at[(group, *index, pl.ds(row, rows), pl.ds(col, cols))]

    def region_small(at, half):
        index = [at[a] if at.get(a) is not None else slice(None) for a in (Z, Y, X)]
        return tiles.at[(*index, slice(None) if half is None else half)]

    def gather_copy(task):
        group, order, axis, kind = task
        axes = ORDERS[order]
        done = axes[: axes.index(axis)]
        at = {a: here[a] for a in (Z, Y, X) if a not in done}
        step = -1 if kind.endswith("-") else 1
        half = None
        if kind[0] == "f":
            at[axis] = beside(axis, -step)
            half = 0 if step == 1 else 1
        sem = GATHER_TASKS[(axes, axis, kind)]
        if group == SMALL:
            ref = region_small(at, half)
            sems = (s.small_s.at[sem], s.small_r.at[sem])
        else:
            row = sum(ROWS[group][:order])
            col, cols = (0, 512) if half is None else (half * 256, 256)
            ref = region(group, at, row, ROWS[group][order], col, cols)
            sems = (s.link_s.at[group, sem], s.gather_r.at[group, sem])
        return send(ref, ref, sems, device(axis, step))

    def reduce_place(group, order, axis, at_axis, half):
        axes = ORDERS[order]
        later = axes[: axes.index(axis)]
        at = {a: here[a] for a in (Z, Y, X) if a not in later}
        at[axis] = at_axis
        row = sum(ROWS[group][:order])
        col, cols = (0, 512) if half is None else (half * 256, 256)
        return at, later, row, ROWS[group][order], col, cols

    def reduce_copy(task):
        _, group, order, axis, kind = task
        step = -1 if kind.endswith("-") else 1
        half = None
        if kind[0] == "h":
            half = 0 if step == 1 else 1
            at_axis = beside(axis, 2)
        else:
            at_axis = beside(axis, step)
        at, _, row, rows, col, cols = reduce_place(group, order, axis, at_axis, half)
        src = region(group, at, row, rows, col, cols)
        buffer = landing[(order, axis, kind)]
        lead = (slice(None),) * (len(buffer.shape) - 3)
        dst = buffer.at[(group, *lead, pl.ds(0, rows))]
        sem = REDUCE_TASKS[(ORDERS[order], axis, kind)]
        sems = (s.link_s.at[group, sem], s.reduce_r.at[group, sem])
        return send(src, dst, sems, device(axis, step))

    def part_copy(number, n):
        sems = (s.part_s.at[number, n], s.part_r.at[number, n])
        rows = span(n, HALF, 16)
        return send(own.at[rows], part.at[number % 2, rows], sems, other_core)

    VEC_SLOT = {Y: 0, Z: 3, X: 6}

    def vec_copy(axis, step):
        slot = 7 if axis == CORE else VEC_SLOT[axis] + step - 1
        where = other_core if axis == CORE else device(axis, step)
        return send(vec, vec_in.at[slot], (s.vec_s.at[slot], s.vec_r.at[slot]), where)

    def copy_of(task):
        if task[0] == PART:
            return part_copy(*task[1:])
        if task[0] == VEC:
            return vec_copy(*task[1:])
        if task[0] == GRADS:
            return reduce_copy(task)
        return gather_copy(task)

    pending = []

    def emit(chains, latency=LATENCY):
        links = {task for chain in chains for step in chain for task, link, _ in step.sends if link is not None}
        links -= {task for task, _, _ in EDGE_TASKS + [CROSS_TASK]}

        def run(step):
            for task in step.waits:
                if task in links:
                    copy_of(task).wait_recv()
            if step.op is not None:
                step.op()
            for task, link, _ in step.sends:
                if task in links:
                    if task[0] not in (PART, VEC):
                        pending.append(task)
                    copy_of(task).start()

        for step in in_order(chains, latency=latency):
            if step.where is None:
                run(step)
            else:
                pl.when(step.where)(lambda: run(step))

    def sent_all():
        for task in pending:
            copy_of(task).wait_send()
        pending.clear()

    def iota(shape, axis):
        return lax.broadcasted_iota(jnp.int32, shape, axis)

    def unpack(chunk):
        rows = tiles[chunk].reshape(256, 128)

        def spread(width, lane_of, dev_of, row_ok):
            lane = iota((128, width), 0)
            pick = (lane == lane_of(iota((128, width), 1))).astype(F32).astype(BF)
            wide = dot(rows, pick)
            i, n = iota((256, width), 0), iota((256, width), 1)
            keep = (i // 16 == dev_of(n)) & row_ok(i % 16, n)
            return jnp.where(keep, wide, 0.0).astype(BF)

        def fold(want, wide):
            a, i = iota((8, 256), 0), iota((8, 256), 1)
            return dot(want(a, i % 16).astype(F32).astype(BF), wide)

        wide = spread(
            1024,
            lambda n: n % 16,
            lambda n: jnp.where((n // 16) % 4 == chunk, n // 64, -1),
            lambda r, n: r < 6,
        )
        sums = fold(lambda a, r: a == r, wide)
        norm_vec[...] = sums if chunk == 0 else norm_vec[...] + sums
        wide = spread(
            128,
            lambda n: (2 * core + n // 64) * 4 + n % 4,
            lambda n: (n % 64) // 4,
            lambda r, n: (r == 6) | (r == 7),
        )
        both_rows = fold(lambda a, r: a == r - 6, wide)
        qv_vec[2 * chunk] = both_rows[0:1]
        qv_vec[2 * chunk + 1] = both_rows[1:2]
        wide = spread(
            512,
            lambda n: 8 * core + n // 64,
            lambda n: (n % 64) // 4,
            lambda r, n: r == 8 + n % 4,
        )
        one_row = fold(lambda a, r: (a == 0) & (r >= 0), wide)
        up_vec[2 * chunk] = one_row[0:1, :256]
        up_vec[2 * chunk + 1] = one_row[0:1, 256:]

    def vector(r):
        return norm_vec[r : r + 1, :]

    def span(i, size, align=None):
        if isinstance(i, int):
            return pl.ds(i * size, size)
        return pl.ds(pl.multiple_of(i * size, align or size), size)

    def tile(t):
        return span(t, TILE, 16)

    def both(number, rows):
        return own[rows, :].astype(F32) + part[number % 2, rows, :].astype(F32)

    def normed(value):
        centred = value - jnp.mean(value, axis=-1, keepdims=True)
        spread = jnp.mean(centred * centred, axis=-1, keepdims=True)
        scale = lax.rsqrt(spread + EPSILON)
        return centred * scale, scale

    def by_n(group, n, cut=slice(None)):
        return jnp.concatenate([w[group, g, n].reshape(256, 512)[:, cut] for g in range(4)], axis=1)

    def add_sum(row, value):
        s.sums[row] += value.reshape(value.shape[0] // 8, 8, D).sum(0)

    head_of = iota((1, 128), 1) // 64
    head_mask = [(head_of == j).astype(F32).astype(BF) for j in range(2)]

    def pick(a, b):
        return jnp.where(iota(a.shape, 1) < 64, a, b)

    def section_copy(slot, t, src):
        rows = tile(t)
        return send(src.at[rows], rows_in.at[slot, rows], (s.sec_s.at[t], s.sec_r.at[t]), other_section)

    def section_cross(slot, t):
        ref = rows_in.at[slot, tile(t)]
        return send(ref, ref, (s.sec_cross_s.at[t], s.sec_cross_r.at[t]), other_core)

    def section_pair(slot, k, use):
        mine, theirs = 2 * k + core, 2 * k + 1 - core
        section_copy(slot, mine, own).wait_recv()
        section_cross(slot, mine).start()
        use(mine)
        section_cross(slot, theirs).wait_recv()
        use(theirs)

    def section_forwarded(slot):
        for k in range(N_TILES // 2):
            section_cross(slot, 2 * k + core).wait_send()

    def section_send(slot, t, src):
        @pl.when(core == lax.rem(t, 2) if not isinstance(t, int) else core == t % 2)
        def _():
            section_copy(slot, t, src).start()

    def section_sent(slot, src):
        for k in range(N_TILES // 2):
            section_copy(slot, 2 * k + core, src).wait_send()

    def result_copy(src, owner):
        micro, owner_core = z // 2, lax.rem(z, 2)
        cols = pl.ds(pl.multiple_of(core * 512, 512), 512)
        from_ref = src.at[pl.ds(owner * TILE, TILE), cols]
        stays = jnp.logical_and(owner == z, core == owner_core)
        where = {CORE: owner_core, TENSOR: jnp.int32(owner)}
        to_ref = out_rows.at[micro, :, cols]
        sems = (s.res_s.at[owner], s.res_r.at[micro, core])
        return stays, send(from_ref, to_ref, sems, where), pltpu.make_async_copy(from_ref, to_ref, sems[1])

    def result_send(src):
        for owner in range(4):
            stays, away, stay = result_copy(src, owner)

            @pl.when(stays)
            def _():
                stay.start()

            @pl.when(jnp.logical_not(stays))
            def _():
                away.start()

    def result_sent(src):
        for owner in range(4):
            stays, away, stay = result_copy(src, owner)

            @pl.when(jnp.logical_not(stays))
            def _():
                away.wait_send()

    def norm_one(t):
        rows = tile(t)
        value, _ = normed(rows_in[0, rows, :].astype(F32))
        h1[rows, :] = (value * vector(0) + vector(1)).astype(BF)

    def project(pair, r):
        rows = span(r, HALF, 16)
        a, b = 2 * pair, 2 * pair + 1
        wa, wb = w[0, a].reshape(D, 512), w[0, b].reshape(D, 512)
        for half, weights in ((a, wa[:, :256]), (b, wb[:, :256])):
            p = dot(h1[rows, :], weights)
            qkv[half, 0, rows] = ((p[:, :128] + qv_vec[2 * half]) * 0.125).astype(BF)
            qkv[half, 1, rows] = p[:, 128:].astype(BF)
        p = dot(h1[rows, :], jnp.concatenate([wa[:, 256:384], wb[:, 256:384]], axis=1))
        qkv[a, 2, rows] = (p[:, :128] + qv_vec[2 * a + 1]).astype(BF)
        qkv[b, 2, rows] = (p[:, 128:] + qv_vec[2 * b + 1]).astype(BF)

    def attend(g):
        query, key, value = qkv[g, 0], qkv[g, 1], qkv[g, 2]
        outs = []
        for j in range(2):
            scores = dot_nt(key * head_mask[j], query)
            e = jnp.exp(scores - jnp.max(scores, axis=0, keepdims=True))
            p = (e * (1.0 / jnp.sum(e, axis=0, keepdims=True))).astype(BF)
            probs[2 * g + j] = p
            outs.append(dot_tn(p, value))
        o[:, span(g, 128)] = pick(*outs).astype(BF)

    def out_part(r, n):
        rows = span(r, HALF, 16)
        own[rows, span(n, 256)] = dot_nt(o[rows, :], by_n(0, n, slice(384, 512))).astype(BF)

    def norm_two(t):
        rows = tile(t)
        middle = rows_in[0, rows, :].astype(F32) + both(0, rows) + vector(2)
        r1[rows, :] = middle
        value, _ = normed(middle)
        h2[rows, :] = (value * vector(3) + vector(4)).astype(BF)

    def feed(i, with_grad=False):
        g, half = (i // 2, i % 2) if isinstance(i, int) else (i // 2, lax.rem(i, 2))
        weights = w[1, g, :, :, :, span(half, 256)].reshape(D, 256)
        for t in range(2):
            rows = pl.ds(t * 288, 288)
            u = dot(h2[rows, :], weights) + up_vec[i]
            phi = 0.5 + 0.5 * lax.erf(u * (2.0**-0.5))
            act[rows, span(i, 256)] = (u * phi).astype(BF)
            slope = phi + u * jnp.exp(u * u * -0.5) * 0.3989422804014327
            if with_grad:
                slope = slope * pull[rows, span(i, 256)].astype(F32)
            slope = slope.astype(BF)
            pull[rows, span(i, 256)] = slope
            if with_grad:
                add_bias(i, t, slope)

    def down(r, n):
        rows = span(r, HALF, 16)
        own[rows, span(n, 256)] = dot_nt(act[rows, :], by_n(2, n)).astype(BF)

    def finish(t):
        rows = tile(t)
        out_b[rows, :] = (r1[rows, :] + both(1, rows) + vector(5)).astype(BF)

    def add_bias(i, r, value):
        value = jnp.sum(value.astype(F32), axis=0, keepdims=True)
        s.up_grad[i] = value if r == 0 else s.up_grad[i] + value

    def feed_grad(i, rows):
        g, half = (i // 2, i % 2) if isinstance(i, int) else (i // 2, lax.rem(i, 2))
        return dot(rows_in[1, rows, :], w[2, g, :, :, :, span(half, 256)].reshape(D, 256))

    def feed_early(i):
        pull[:, span(i, 256)] = feed_grad(i, slice(None)).astype(BF)

    def feed_back(r, i):
        rows = pl.ds(r * HALF, HALF)
        du = (feed_grad(i, rows) * pull[rows, span(i, 256)].astype(F32)).astype(BF)
        pull[rows, span(i, 256)] = du
        add_bias(i, r, du)

    def up_back(r, n):
        rows = span(r, HALF, 16)
        own[rows, span(n, 256)] = dot_nt(pull[rows, :], by_n(1, n)).astype(BF)

    def norm_back(value, grad, gain, gain_row, shift_row):
        hat, scale = normed(value)
        add_sum(gain_row, grad * hat)
        add_sum(shift_row, grad)
        dy = grad * gain
        return scale * (
            dy - jnp.mean(dy, axis=-1, keepdims=True) - hat * jnp.mean(dy * hat, axis=-1, keepdims=True)
        )

    def norm_two_back(t):
        rows = tile(t)
        pulled = norm_back(r1[rows, :], both(2, rows), vector(3), 3, 4)
        gy = rows_in[1, rows, :].astype(F32)
        grad = gy + pulled
        add_sum(5, gy)
        add_sum(2, grad)
        r1[rows, :] = grad
        gr[rows, :] = grad.astype(BF)

    def out_back(pair):
        weights = [w[0, 2 * pair + j, :, :, :, 384:512].reshape(D, 128) for j in range(2)]
        do[:, span(pair, 256)] = dot(gr[...], jnp.concatenate(weights, axis=1)).astype(BF)

    def attend_back(g):
        query, key, value = qkv[g, 0], qkv[g, 1], qkv[g, 2]
        grad = do[:, span(g, 128)]
        dq, dk, dv = [], [], []
        for j in range(2):
            p = probs[2 * g + j]
            dv.append(dot(p, grad))
            dp = dot_nt(value * head_mask[j], grad)
            p = p.astype(F32)
            ds = (p * (dp - jnp.sum(dp * p, axis=0, keepdims=True))).astype(BF)
            dk.append(dot(ds, query))
            dq.append(dot_tn(ds, key))
        dq, dk, dv = (pick(*pair).astype(BF) for pair in (dq, dk, dv))
        dq = dq * jnp.asarray(0.125, BF)
        qkv[g, 0] = dq
        qkv[g, 1] = dk
        qkv[g, 2] = dv
        s.qv_grad[2 * g] = jnp.sum(dq.astype(F32), axis=0, keepdims=True)
        s.qv_grad[2 * g + 1] = jnp.sum(dv.astype(F32), axis=0, keepdims=True)

    def qkv_all(first_g, last_g, rows=slice(None)):
        return jnp.concatenate([qkv[g, k, rows] for g in range(first_g, last_g) for k in range(3)], axis=1)

    def project_back(r, n):
        rows = span(r, HALF, 16)
        own[rows, span(n, 256)] = dot_nt(qkv_all(0, 4, rows), by_n(0, n, slice(0, 384))).astype(BF)

    def norm_one_back(t):
        rows = tile(t)
        pulled = norm_back(rows_in[0, rows, :].astype(F32), both(3, rows), vector(0), 0, 1)
        own[rows, :] = (r1[rows, :] + pulled).astype(BF)

    def zero_sums():
        s.sums[...] = jnp.zeros_like(s.sums)

    def fill_vec():
        vec[...] = jnp.zeros_like(vec)
        for r in range(6):
            vec[r : r + 1, :] = jnp.sum(s.sums[r], axis=0, keepdims=True)
        for r in range(8):
            vec[8 + r : 9 + r, 512:640] = s.qv_grad[r]
            vec[8 + r // 2 : 9 + r // 2, r % 2 * 256 : r % 2 * 256 + 256] = s.up_grad[r]

    def grads(group, m):
        def left(ref):
            return ref[:, m * 256 : m * 256 + 256].T

        def put(g, col, value):
            cols = value.shape[1]
            w[group, g, m, :, :, col : col + cols] = value.astype(BF).reshape(2, 128, cols)

        if group == 0:
            first_left = left(h1)
            for pair in range(2):
                out = dot(first_left, qkv_all(2 * pair, 2 * pair + 2))
                put(2 * pair, 0, out[:, :384])
                put(2 * pair + 1, 0, out[:, 384:])
        else:
            rows, right = (h2, pull) if group == 1 else (rows_in.at[1], act)
            rows_t = left(rows)
            for g in range(4):
                put(g, 0, dot(rows_t, right[:, g * 512 : g * 512 + 512]))

    def out_grads(m):
        out = dot(gr[:, m * 256 : m * 256 + 256].T, o[...]).astype(BF)
        for g in range(4):
            w[0, g, m, :, :, 384:512] = out[:, g * 128 : g * 128 + 128].reshape(2, 128, 128)

    def half_steps(number, body, cost, waits):
        return [
            Step(
                waits if (r, n) == (0, 0) else [],
                cost,
                [((PART, number, r), CORE, 590000)] if n == 3 else (),
                partial(body, r, n),
            )
            for r in range(2)
            for n in range(4)
        ]

    def norm_steps(number, body, cost, after=None):
        def one(t, pieces):
            for n in pieces:
                part_copy(number, n).wait_send()
            body(t)
            if after is not None:
                after(t)

        steps = []
        for t in range(N_TILES):
            pieces = [t // 2] if t % 2 == 0 else []
            steps.append(Step([(PART, number, n) for n in pieces], cost, (), partial(one, t, pieces)))
        return steps

    def everything(group):
        return [(group, order) for order in range(4)]

    forward = []
    forward += [Step([(READY, 1)] if t == 0 else [], 0.5, (), partial(norm_one, t)) for t in range(N_TILES)]
    forward += [Step(everything(0), 0.7, (), partial(project, p, r)) for p in range(2) for r in range(2)]
    forward += [Step([], 1.6, (), partial(attend, g)) for g in range(4)]
    forward += half_steps(0, out_part, 0.2, [])
    forward += norm_steps(0, norm_two, 0.6)
    forward += [Step(everything(1), 0.6, (), partial(feed, i)) for i in range(8)]
    forward += half_steps(1, down, 0.5, everything(2))
    forward += norm_steps(1, finish, 0.3, lambda t: section_send(0, t, out_b))
    forward = [step._replace(where=first) for step in forward]
    unpacking = [Step([(SMALL, 0)], 1.5, (), partial(unpack, chunk)) for chunk in range(4)]
    edge_steps = [
        Step([], 0.2, EDGE_TASKS, edge_start),
        Step([(0, 3)], 0.2, [CROSS_TASK], edge_arrived),
        Step([CROSS_TASK[0]], 0.2, [note(READY, 1)], edge_done),
    ]
    gathers = [gather_chain(SMALL, 0)] + [gather_chain(g, o) for g in range(3) for o in range(4)]
    emit(gathers + [edge_steps, unpacking + forward])
    sent_all()

    def loop(count, body):
        def one(i, carry):
            body(i)
            return carry

        lax.fori_loop(0, count, one, 0)

    zero_sums()

    def exchange_halves(number, body, use):
        for r in range(2):
            loop(4, partial(body, r))
            part_copy(number, r).start()
        for r in range(2):
            part_copy(number, r).wait()
            loop(2, lambda t: use(2 * r + t))

    @pl.when(sec == 1)
    def _():
        loop(8, feed_early)
        for k in range(N_TILES // 2):
            section_pair(0, k, norm_one)
            loop(2, lambda pair: project(pair, k))
        loop(4, attend)
        exchange_halves(0, out_part, norm_two)
        loop(8, partial(feed, with_grad=True))
        exchange_halves(1, down, finish)
        result_send(out_b)
        exchange_halves(2, up_back, norm_two_back)
        loop(2, out_back)
        loop(4, attend_back)

        def last(t):
            norm_one_back(t)
            section_send(1, t, own)

        exchange_halves(3, project_back, last)
        section_forwarded(0)

    def reduce_add(group, order, op):
        axis, kind = op
        if kind == "end":
            kinds = ("s",) if axis == X else ("s+", "s-")
            at_axis, half = here[axis], None
        else:
            kinds = (kind,)
            at_axis = beside(axis, 1 if kind == "h+" else -1)
            half = 0 if kind == "h+" else 1
        at, later, row, rows, col, cols = reduce_place(group, order, axis, at_axis, half)
        open_axes = [a for a in (Z, Y, X) if a in later]
        count = 1
        for a in open_axes:
            count *= SIZE[a]

        def one(i):
            rest, index = i, dict(at)
            for a in reversed(open_axes):
                index[a] = lax.rem(rest, SIZE[a])
                rest = rest // SIZE[a]
            lead = tuple(index[a] for a in open_axes)
            place = (group, index[Z], index[Y], index[X], pl.ds(row, rows), pl.ds(col, cols))
            value = w[place].astype(F32)
            for k in kinds:
                value += landing[(order, axis, k)][(group, *lead, pl.ds(0, rows), slice(None))].astype(F32)
            if later or kind != "end":
                w[place] = value.astype(BF)
            else:
                total[group, pl.ds(row, rows), :] = value

        if count == 1:
            one(0)
        else:
            loop(count, one)

    def vec_add(axis):
        value = vec[...]
        for step in range(1, SIZE[axis]):
            vec_copy(axis, step).wait_send()
            value += vec_in[VEC_SLOT[axis] + step - 1]
        vec[...] = value
        if axis == X:
            out_vectors[0] = value

    def vec_last():
        vec_copy(CORE, 1).wait_send()
        out_vectors[1] = vec_in[7]

    def vec_tasks(axis):
        return [((VEC, axis, step), VEC, 100000) for step in range(1, SIZE[axis])]

    def vec_waits(axis):
        return [(VEC, axis, step) for step in range(1, SIZE[axis])]

    vec_chain = [
        Step([(READY, 4)], 0.3, vec_tasks(Y), fill_vec),
        Step(vec_waits(Y), 0.2, vec_tasks(Z), lambda: vec_add(Y)),
        Step(vec_waits(Z), 0.2, vec_tasks(X), lambda: vec_add(Z)),
        Step(vec_waits(X), 0.2, [((VEC, CORE, 1), CORE, 65536)], lambda: vec_add(X)),
        Step([(VEC, CORE, 1)], 0.1, (), vec_last),
    ]

    def final_copy(group):
        src = total.at[group, pl.ds(pl.multiple_of((1 - core) * 64, 64), 64), :]
        return send(src, out_weights.at[group, core], (s.fin_s.at[group], s.fin_r.at[group]), other_core)

    def final_local(group):
        src = total.at[group, pl.ds(pl.multiple_of(core * 64, 64), 64), :]
        return pltpu.make_async_copy(src, out_weights.at[group, core], s.local.at[group])

    def final_start(group):
        final_copy(group).start()
        final_local(group).start()

    finals = [
        [Step([(TOTAL, group, order) for order in range(4)], 0.1, (), partial(final_start, group))]
        for group in (2, 1, 0)
    ]

    def only_first(steps):
        return [step._replace(where=first) for step in steps]

    def grad_steps(group, cost):
        return [
            Step([], cost, [note(GRADS, group)] if m == 3 else (), partial(grads, group, m)) for m in range(4)
        ]

    backward = []
    for k in range(N_TILES // 2):
        backward += only_first([Step([], 0.0, (), partial(section_pair, 1, k, lambda t: None))])
        backward += only_first([Step([], 0.25, (), partial(feed_back, k, i)) for i in range(8)])
    backward += only_first([Step([], 0.0, (), partial(section_forwarded, 1))])
    backward += grad_steps(2, 0.9)
    backward += only_first(half_steps(2, up_back, 0.4, []))
    backward += grad_steps(1, 1.0)
    backward += only_first(norm_steps(2, norm_two_back, 0.8))
    backward += only_first([Step([], 0.5, (), partial(out_back, p)) for p in range(2)])
    backward += only_first([Step([], 2.0, (), partial(attend_back, g)) for g in range(4)])
    backward += only_first(half_steps(3, project_back, 0.35, []))
    backward += [Step([], 0.5, (), partial(out_grads, m)) for m in range(4)]
    backward += grad_steps(0, 1.0)
    backward += only_first(norm_steps(3, norm_one_back, 0.8))
    backward += only_first([Step([], 0.1, (), lambda: result_send(own))])
    backward += [Step([], 0.0, [note(READY, 4)])]
    reduces = [reduce_chain(g, o, reduce_add) for g in (2, 1, 0) for o in range(4)]
    emit(reduces + finals + [vec_chain, backward], latency=3.0)
    sent_all()

    for group in range(3):
        final_local(group).wait()
        final_copy(group).wait()

    @pl.when(first)
    def _():
        section_sent(0, out_b)
        result_sent(own)

    @pl.when(sec == 1)
    def _():
        section_sent(1, own)
        result_sent(out_b)

    for micro in range(2):
        for half in range(2):
            dst = out_rows.at[micro, :, pl.ds(half * 512, 512)]
            pltpu.make_async_copy(dst, dst, s.res_r.at[micro, half]).wait()


def dma(*shape):
    return pltpu.SemaphoreType.DMA(shape)


SCRATCH = dict(
    blocks=pltpu.VMEM((2, 3, 64, 512), BF),
    w=pltpu.VMEM((3, 4, 4, 2, 128, 512), BF),
    rows_in=pltpu.VMEM((2, T, D), BF),
    h1=pltpu.VMEM((T, D), BF),
    h2=pltpu.VMEM((T, D), BF),
    qkv=pltpu.VMEM((4, 3, T, 128), BF),
    o=pltpu.VMEM((T, 512), BF),
    r1=pltpu.VMEM((T, D), F32),
    act=pltpu.VMEM((T, 2048), BF),
    pull=pltpu.VMEM((T, 2048), BF),
    probs=pltpu.VMEM((8, T, T), BF),
    part=pltpu.VMEM((2, T, D), BF),
    own=pltpu.VMEM((T, D), BF),
    out_b=pltpu.VMEM((T, D), BF),
    gr=pltpu.VMEM((T, D), BF),
    do=pltpu.VMEM((T, 512), BF),
    tiles=pltpu.VMEM((4, 4, 2, 2, 16, 128), BF),
    norm_vec=pltpu.VMEM((8, D), F32),
    qv_vec=pltpu.VMEM((8, 1, 128), F32),
    up_vec=pltpu.VMEM((8, 1, 256), F32),
    sums=pltpu.VMEM((6, 8, D), F32),
    qv_grad=pltpu.VMEM((8, 1, 128), F32),
    up_grad=pltpu.VMEM((8, 1, 256), F32),
    vec=pltpu.VMEM((16, D), F32),
    vec_in=pltpu.VMEM((8, 16, D), F32),
    total=pltpu.VMEM((3, 128, 512), F32),
    local=dma(4),
    swap_s=dma(4),
    swap_r=dma(4),
    edge_s=dma(2, 2),
    edge_r=dma(4),
    cross=dma(2),
    small_s=dma(N_SMALL),
    small_r=dma(N_SMALL),
    link_s=dma(3, N_TASKS),
    gather_r=dma(3, N_TASKS),
    reduce_r=dma(3, N_TASKS),
    part_s=dma(4, 2),
    part_r=dma(4, 2),
    sec_s=dma(N_TILES),
    sec_r=dma(N_TILES),
    sec_cross_s=dma(N_TILES),
    sec_cross_r=dma(N_TILES),
    res_s=dma(4),
    res_r=dma(2, 2),
    vec_s=dma(8),
    vec_r=dma(8),
    fin_s=dma(3),
    fin_r=dma(3),
)


def finish_kernel(rows, weights, vectors, ends, qkv, qv, out, up, up_bias, down, norm):
    core, z = lax.axis_index(CORE), lax.axis_index(TENSOR)
    position = (lax.axis_index(DP_Y) * 2 + lax.axis_index(DP_X)) * 2 + core
    ends[...] = rows[...].astype(F32)
    for half in range(2):
        narrow, wide = slice(half * 128, half * 128 + 128), slice(half * 512, half * 512 + 512)
        for k in range(3):
            qkv[k, :, narrow] = weights[0, half, :, k * 128 : k * 128 + 128]
        out[:, narrow] = weights[0, half, :, 384:512]
        up[:, wide] = weights[1, half]
        down[:, wide] = weights[2, half]
    mine = pltpu.roll(vectors[0], D - (position * 4 + z) * 16, 1)
    for r in range(6):
        norm[r] = mine[r : r + 1, :16]
    bias = jnp.zeros((8, 128), F32)
    for half in range(2):
        own = jnp.where(core == half, vectors[0], vectors[1])
        heads = pltpu.roll(pltpu.roll(own[8:16, 512:640], 128 - position * 4, 1), 8 - 2 * z, 0)
        hidden = pltpu.roll(pltpu.roll(own[8:16, :512], 512 - position * 4, 1), 8 - z, 0)
        for j in range(2):
            for part in range(2):
                qv[part, 2 * half + j : 2 * half + j + 1, :] = heads[part : part + 1, 64 * j : 64 * j + 4]
        row, lane = (lax.broadcasted_iota(jnp.int32, (8, 512), i) for i in range(2))
        spread = jnp.where(lane % 64 == row, jnp.broadcast_to(hidden[0:1], (8, 512)), 0.0)
        lane, column = (lax.broadcasted_iota(jnp.int32, (512, 128), i) for i in range(2))
        gather = (lane // 64 + 8 * half == column).astype(F32)
        bias += jnp.dot(spread, gather, precision=lax.Precision.HIGHEST, preferred_element_type=F32)
    up_bias[...] = bias[:4, :16]


def body(boundary, w_qkv, qv_bias, w_out, up_weight, up_bias, down_weight, norm_bias):
    anywhere = pl.BlockSpec(memory_space=pl.ANY)
    vmem = pl.BlockSpec(memory_space=pltpu.VMEM)
    small = jnp.concatenate([norm_bias[0], qv_bias[0].reshape(2, 16), up_bias[0].T])
    small = jnp.pad(small, ((0, 4), (0, 112)))
    results = pl.pallas_call(
        kernel,
        out_shape=(
            jax.ShapeDtypeStruct((2, TILE, D), BF),
            jax.ShapeDtypeStruct((3, 2, 64, 512), F32),
            jax.ShapeDtypeStruct((2, 16, D), F32),
        ),
        in_specs=[anywhere] + [vmem] * 5,
        out_specs=(anywhere, anywhere, vmem),
        scratch_shapes=[*SCRATCH.values(), *(pltpu.VMEM(shape, BF) for shape in LANDINGS.values())],
        compiler_params=pltpu.CompilerParams(
            collective_id=0, has_side_effects=True, vmem_limit_bytes=62 << 20
        ),
    )(boundary[0, :, 0], small, jnp.moveaxis(w_qkv[0], 1, 0), w_out[0].T, up_weight[0], down_weight[0].T)
    shapes = ((2, TILE, D), (3, 64, 256), (2, 4, 4), (64, 256), (64, 1024), (4, 16), (64, 1024), (6, 1, 16))
    ends, qkv, qv, out, up, up_bias_grad, down, norm = pl.pallas_call(
        finish_kernel,
        out_shape=tuple(jax.ShapeDtypeStruct(shape, F32) for shape in shapes),
        in_specs=[vmem] * 3,
        out_specs=(vmem,) * 8,
    )(*results)
    results = (jnp.moveaxis(qkv, 0, 1), qv, out.T, up, up_bias_grad.T, down.T, norm[:, 0])
    return (ends[None, :, None], *(result[None] for result in results))


def solution(mesh):
    torus = Mesh(mesh.devices.reshape(mesh.shape[SECTION], 4, 2, 2, mesh.shape[TENSOR]), AXES)
    in_specs = (
        P(SECTION, None, DP, TENSOR, None),
        P(SECTION, DP, None, TENSOR),
        P(SECTION, None, TENSOR, DP),
        P(SECTION, TENSOR, DP),
        P(SECTION, DP, TENSOR),
        P(SECTION, TENSOR, DP),
        P(SECTION, TENSOR, DP),
        P(SECTION, None, DP_TENSOR),
    )
    return jax.shard_map(body, mesh=torus, in_specs=in_specs, out_specs=in_specs, check_vma=False)
```
